128 devices in a mesh: dp: 2 (over core), context: 8 (over z, x_hi), experts: 8 (over x_lo, y).
Axes of the slice: x: 4 (x_hi: 2, x_lo: 2; x = x_hi * 2 + x_lo), y: 4, z: 4, core: 2. Of those that a mesh axis runs over, the one named last changes fastest.
Arguments:
- tokens: bfloat16 [16, 1024, 1536], P(('dp', 'experts'), 'context'), may hold values from -6 to 6
- cotangent: bfloat16 [16, 1024, 1536], P(('dp', 'experts'), 'context'), may hold values from -6 to 6
- expert_ids: int32 [2, 16, 1024, 4], P(None, ('dp', 'experts'), 'context'), may hold values from 0 to 15, all different within a row; in each aligned block of 128 rows (0 to 127, 128 to 255, ..., all dimensions but the last counted through in order) at most 40 rows name the same one
- gate_values: float32 [2, 16, 1024, 4], P(None, ('dp', 'experts'), 'context'), may hold values from 0.1 to 0.4
- block_order: int32 [16, 8], P(('dp', 'experts')), may hold values from 0 to 7, each once within a row
- qkv_weight: float32 [2, 1536, 2048], P(None, ('dp', 'context', 'experts')), may hold values from -0.15625 to 0.15625
- qkv_first: float32 [2, 1536, 2048], P(None, ('dp', 'context', 'experts'))
- qkv_second: float32 [2, 1536, 2048], P(None, ('dp', 'context', 'experts')), as said below
- out_weight: float32 [2, 1536, 1536], P(None, None, ('dp', 'context', 'experts')), may hold values from -0.625 to 0.625
- out_first: float32 [2, 1536, 1536], P(None, None, ('dp', 'context', 'experts'))
- out_second: float32 [2, 1536, 1536], P(None, None, ('dp', 'context', 'experts')), as said below
- in_weight: float32 [2, 16, 1536, 1536], P(None, 'experts', ('dp', 'context')), may hold values from -0.15625 to 0.15625
- in_first: float32 [2, 16, 1536, 1536], P(None, 'experts', ('dp', 'context'))
- in_second: float32 [2, 16, 1536, 1536], P(None, 'experts', ('dp', 'context')), as said below
- down_weight: float32 [2, 16, 768, 1536], P(None, 'experts', None, ('dp', 'context')), may hold values from -0.4375 to 0.4375
- down_first: float32 [2, 16, 768, 1536], P(None, 'experts', None, ('dp', 'context'))
- down_second: float32 [2, 16, 768, 1536], P(None, 'experts', None, ('dp', 'context')), as said below
- norm_gains: float32 [2, 2, 1536], P(None, None, ('dp', 'context', 'experts')), may hold values from 0.5 to 1.5
- gain_first: float32 [2, 2, 1536], P(None, None, ('dp', 'context', 'experts'))
- gain_second: float32 [2, 2, 1536], P(None, None, ('dp', 'context', 'experts')), as said below
Outputs:
- result: bfloat16 [16, 1024, 1536], P(('dp', 'experts'), 'context')
- input_grad: float32 [16, 1024, 1536], P(('dp', 'experts'), 'context')
- qkv_new: float32 [2, 1536, 2048], P(None, ('dp', 'context', 'experts'))
- qkv_first_new: float32 [2, 1536, 2048], P(None, ('dp', 'context', 'experts'))
- qkv_second_new: float32 [2, 1536, 2048], P(None, ('dp', 'context', 'experts'))
- out_new: float32 [2, 1536, 1536], P(None, None, ('dp', 'context', 'experts'))
- out_first_new: float32 [2, 1536, 1536], P(None, None, ('dp', 'context', 'experts'))
- out_second_new: float32 [2, 1536, 1536], P(None, None, ('dp', 'context', 'experts'))
- in_new: float32 [2, 16, 1536, 1536], P(None, 'experts', ('dp', 'context'))
- in_first_new: float32 [2, 16, 1536, 1536], P(None, 'experts', ('dp', 'context'))
- in_second_new: float32 [2, 16, 1536, 1536], P(None, 'experts', ('dp', 'context'))
- down_new: float32 [2, 16, 768, 1536], P(None, 'experts', None, ('dp', 'context'))
- down_first_new: float32 [2, 16, 768, 1536], P(None, 'experts', None, ('dp', 'context'))
- down_second_new: float32 [2, 16, 768, 1536], P(None, 'experts', None, ('dp', 'context'))
- gains_new: float32 [2, 2, 1536], P(None, None, ('dp', 'context', 'experts'))
- gains_first_new: float32 [2, 2, 1536], P(None, None, ('dp', 'context', 'experts'))
- gains_second_new: float32 [2, 2, 1536], P(None, None, ('dp', 'context', 'experts'))
The draws below stay inside these ranges and needn't reach their ends.
Inputs may be any that keep to these rules, and one draw needn't show every extreme that they name: `expert_ids`: each row names 4 different experts. In each layer, the 128 rows that one device holds (aligned blocks) name no expert more than 40 times; in some blocks an expert is named exactly 40 times. Each row is a permutation: the device at place c of context holds block block_order[s, c] of sequence s, tokens block_order[s, c] * 128 to block_order[s, c] * 128 + 127, and tokens, cotangent, expert_ids and gate_values store the blocks in that order. `qkv_second`: positive. `out_second`: positive. `in_second`: positive. `down_second`: positive. `gain_second`: positive.
All inputs are finite; a program needn't handle non-finite values.
Results may differ from the reference program's by a relative error of at most 0.024.
Values may be sent and summed in bfloat16 or wider, within the bound.
No kernel may reach another device: no remote copies, remote signals or barrier semaphores. Data moves between devices by JAX's collectives and lax.ppermute only.
A program may use at most 384 MiB of HBM per device.

```python
import math
import jax
import jax.numpy as jnp
import numpy as np
from jax import lax

D = 1536
HQ = 12
HK = 2
HD = 128
FF = 768
TOP = 4
TOK_DEV = 128
LAYERS = 2
STEP = 5
EXPERTS = 16
CAP = 40
LENGTH = 1024
SEQS = 16
N_CONTEXT = 8


def gradient_sizes():
    total = float(SEQS * LENGTH)
    per_expert = total * TOP / EXPERTS
    share = 3.0 * math.log(LENGTH) / LENGTH
    table = [None] * LAYERS
    upstream = 1.0
    for layer in reversed(range(LAYERS)):
        d_ret = 0.265 * upstream
        d_hid = d_ret * 2.0 * math.sqrt(D / FF)
        d_both = 0.65 * d_hid
        down_size = 0.65 * d_ret * math.sqrt(per_expert)
        in_size = d_both * math.sqrt(per_expert)
        d_ffn = math.sqrt(TOP) * d_both
        gain_ffn = d_ffn * math.sqrt(total)
        middle = math.sqrt(upstream ** 2 + d_ffn ** 2)
        d_mix = middle * math.sqrt(16.0 * D / (HQ * HD))
        out_size = math.sqrt(share) * middle * math.sqrt(total)
        query_rms = d_mix * math.sqrt(share)
        pair_rms = d_mix * math.sqrt(2.5 * (HQ // HK) * share)
        d_attn = math.sqrt((HQ * HD * query_rms ** 2 + 2 * HK * HD * pair_rms ** 2) / D)
        gain_attn = d_attn * math.sqrt(total)
        table[layer] = (query_rms * math.sqrt(total), pair_rms * math.sqrt(total), out_size, in_size, down_size, gain_attn, gain_ffn)
        upstream = math.sqrt(middle ** 2 + d_attn ** 2)
    return table


def state_draw(key, shape, scales, second):
    if second:
        factor = jnp.exp(jax.random.uniform(key, shape, jnp.float32, 0.0, math.log(4.0)))
        return (scales * scales * (0.05 / 0.95) * factor).astype(jnp.float32)
    values = jnp.clip(jax.random.normal(key, shape, jnp.float32), -4.0, 4.0)
    return (values * scales * (0.1 / 0.9)).astype(jnp.float32)


def layer_scales(index):
    table = gradient_sizes()
    return jnp.array([row[index] for row in table], jnp.float32)


def qkv_scales():
    table = gradient_sizes()
    column = jnp.arange((HQ + 2 * HK) * HD)
    rows = [jnp.where(column < HQ * HD, row[0], row[1]).astype(jnp.float32) for row in table]
    return jnp.stack(rows)[:, None, :]


def gain_scales():
    table = gradient_sizes()
    return jnp.array([[row[5], row[6]] for row in table], jnp.float32)[:, :, None]


def draw_qkv_first(key, part):
    key = jax.random.fold_in(key, 11)
    return state_draw(key, (LAYERS, D, (HQ + 2 * HK) * HD), qkv_scales(), False)


def draw_qkv_second(key, part):
    key = jax.random.fold_in(key, 12)
    return state_draw(key, (LAYERS, D, (HQ + 2 * HK) * HD), qkv_scales(), True)


def draw_out_first(key, part):
    key = jax.random.fold_in(key, 21)
    return state_draw(key, (LAYERS, HQ * HD, D), layer_scales(2)[:, None, None], False)


def draw_out_second(key, part):
    key = jax.random.fold_in(key, 22)
    return state_draw(key, (LAYERS, HQ * HD, D), layer_scales(2)[:, None, None], True)


def draw_in_first(key, part):
    key = jax.random.fold_in(key, 31)
    return state_draw(key, (LAYERS, EXPERTS, D, 2 * FF), layer_scales(3)[:, None, None, None], False)


def draw_in_second(key, part):
    key = jax.random.fold_in(key, 32)
    return state_draw(key, (LAYERS, EXPERTS, D, 2 * FF), layer_scales(3)[:, None, None, None], True)


def draw_down_first(key, part):
    key = jax.random.fold_in(key, 41)
    return state_draw(key, (LAYERS, EXPERTS, FF, D), layer_scales(4)[:, None, None, None], False)


def draw_down_second(key, part):
    key = jax.random.fold_in(key, 42)
    return state_draw(key, (LAYERS, EXPERTS, FF, D), layer_scales(4)[:, None, None, None], True)


def draw_gain_first(key, part):
    key = jax.random.fold_in(key, 51)
    return state_draw(key, (LAYERS, 2, D), gain_scales(), False)


def draw_gain_second(key, part):
    key = jax.random.fold_in(key, 52)
    return state_draw(key, (LAYERS, 2, D), gain_scales(), True)


def shard_levels(own_key, dims, cuts, smallest, high):
    level, own = 1.0, jax.random.fold_in(own_key, 6)
    for dim, shards_of in cuts:
        heights = jnp.exp(jax.random.uniform(jax.random.fold_in(own, dim), (shards_of,), jnp.float32, smallest / len(cuts), high / len(cuts)))
        level = level * jnp.repeat(heights, dims[dim] // shards_of).reshape([-1 if axis == dim else 1 for axis in range(len(dims))])
    return level


def assign_block(stream_key, own, number, rows, amount, top, bound, slope):
    ranking = jax.random.permutation(stream_key, amount)
    crowded, usual = load_shares(amount, rows * top, bound, slope, True), load_shares(amount, rows * top, bound, slope, False)
    places = jnp.arange(amount)

    def named(sizes, turn):
        used = int((sizes > 0).sum())
        fixed = max(1, used // 4)
        passed = fixed + (places - fixed + turn * (used - fixed)) % max(1, amount - fixed)
        return jnp.zeros((amount,), jnp.int32).at[ranking[jnp.where(places < fixed, places, passed)]].set(jnp.asarray(sizes, jnp.int32))

    sizes = jnp.where(number % 4 == 0, named(crowded, number // 4), named(usual, number - number // 4 - 1))
    mixed = jax.random.permutation(jax.random.fold_in(own, 3), amount)
    donor, taker = mixed[0:amount // 2 * 2:2], mixed[1:amount // 2 * 2:2]
    margin = jnp.minimum(sizes[donor] - 1, bound - sizes[taker]) // 2
    margin = jnp.where((donor == ranking[0]) | (taker == ranking[0]) | (sizes[taker] == 0), 0, jnp.maximum(margin, 0))
    passed = jax.random.randint(jax.random.fold_in(own, 4), (amount // 2,), 0, 1 << 20) % (margin + 1)
    sizes = sizes.at[donor].add(-passed).at[taker].add(passed)
    items = jnp.searchsorted(jnp.cumsum(sizes), jnp.arange(rows * top), side="right").astype(jnp.int32)
    table = items.reshape(top, rows).T
    table = table[jax.random.permutation(jax.random.fold_in(own, 1), rows)]
    turn = jax.random.randint(jax.random.fold_in(own, 2), (rows, 1), 0, top)
    return jnp.take_along_axis(table, (jnp.arange(top)[None, :] + turn) % top, axis=1)


def load_shares(amount, total, bound, skew, full):
    weights = [(1 << 20) // math.isqrt(standing ** skew) + 1 for standing in range(1, amount + 1)]
    largest = bound if full else min(bound, max(-(-total // amount), total * weights[0] // sum(weights)))
    least = 1 if total - largest >= amount - 1 else 0
    holding, rest = [largest] + [least] * (amount - 1), total - largest - least * (amount - 1)
    while rest > 0:
        movable = [i for i in range(1, amount) if holding[i] < largest] or [i for i in range(1, amount) if holding[i] < bound]
        whole, remaining = sum([weights[i] for i in movable]), rest
        for i in movable:
            more = min(bound - holding[i], max(1, remaining * weights[i] // whole), rest)
            holding[i] = holding[i] + more
            rest = rest - more
    return np.array(holding)


def centred(rng, shape, spread, reach, shards=(), kind=jnp.bfloat16):
    values = jax.random.normal(rng, shape, jnp.float32) * spread
    if len(shards) > 0:
        values = shard_levels(rng, shape, shards, -0.22, 0.18) * values
    return jnp.clip(values, min=-reach, max=reach).astype(kind)


def setup_inputs(seed: int = 0) -> dict:
    arg_keys = jax.random.split(jax.random.key(seed), 21)
    tokens = centred(arg_keys[0], (SEQS, LENGTH, D), 1.0, 6.0, ((0, 16), (1, 8)))
    cotangent = centred(arg_keys[1], (SEQS, LENGTH, D), 1.0, 6.0, ((0, 16), (1, 8)))
    expert_ids_keys = jax.random.split(jax.random.fold_in(arg_keys[2], 1), LAYERS * SEQS * LENGTH // TOK_DEV)
    expert_ids_turns = jax.random.permutation(jax.random.fold_in(arg_keys[2], 3), LAYERS * SEQS * LENGTH // TOK_DEV)
    expert_ids = jax.vmap(lambda own, number: assign_block(jax.random.fold_in(arg_keys[2], 2), own, number, TOK_DEV, EXPERTS, TOP, CAP, 2))(expert_ids_keys, expert_ids_turns).reshape((LAYERS, SEQS, LENGTH, TOP))
    gate_values = jnp.clip(0.1 + 0.3 * jax.random.uniform(arg_keys[3], (LAYERS, SEQS, LENGTH, TOP), jnp.float32) ** shard_levels(arg_keys[3], (LAYERS, SEQS, LENGTH, TOP), ((1, 16), (2, 8)), -0.2, 0.2), 0.1, 0.4)
    block_order = jax.vmap(lambda own: jax.random.permutation(own, N_CONTEXT))(jax.random.split(arg_keys[4], SEQS)).reshape((SEQS, N_CONTEXT)).astype(jnp.int32)
    qkv_weight = centred(arg_keys[5], (LAYERS, D, (HQ + 2 * HK) * HD), D ** -0.5, 0.15625, ((1, 128),), jnp.float32)
    qkv_first = draw_qkv_first(jax.random.fold_in(arg_keys[20], 71), 0)
    qkv_second = draw_qkv_second(jax.random.fold_in(arg_keys[20], 71), 0)
    out_weight = centred(arg_keys[8], (LAYERS, HQ * HD, D), (HQ * HD // 16) ** -0.5, 0.625, ((2, 128),), jnp.float32)
    out_first = draw_out_first(jax.random.fold_in(arg_keys[20], 71), 0)
    out_second = draw_out_second(jax.random.fold_in(arg_keys[20], 71), 0)
    in_weight = centred(arg_keys[11], (LAYERS, EXPERTS, D, 2 * FF), D ** -0.5, 0.15625, ((1, 8), (2, 16)), jnp.float32)
    in_first = draw_in_first(jax.random.fold_in(arg_keys[20], 71), 0)
    in_second = draw_in_second(jax.random.fold_in(arg_keys[20], 71), 0)
    down_weight = centred(arg_keys[14], (LAYERS, EXPERTS, FF, D), (FF // 4) ** -0.5, 0.4375, ((1, 8), (3, 16)), jnp.float32)
    down_first = draw_down_first(jax.random.fold_in(arg_keys[20], 71), 0)
    down_second = draw_down_second(jax.random.fold_in(arg_keys[20], 71), 0)
    norm_gains = jnp.clip(1.0 + 0.1 * jax.random.normal(arg_keys[17], (LAYERS, 2, D), jnp.float32), 0.5, 1.5)
    gain_first = draw_gain_first(jax.random.fold_in(arg_keys[20], 71), 0)
    gain_second = draw_gain_second(jax.random.fold_in(arg_keys[20], 71), 0)
    return dict(tokens=tokens, cotangent=cotangent, expert_ids=expert_ids, gate_values=gate_values, block_order=block_order, qkv_weight=qkv_weight, qkv_first=qkv_first, qkv_second=qkv_second, out_weight=out_weight, out_first=out_first, out_second=out_second, in_weight=in_weight, in_first=in_first, in_second=in_second, down_weight=down_weight, down_first=down_first, down_second=down_second, norm_gains=norm_gains, gain_first=gain_first, gain_second=gain_second)


beta_first = 0.9
beta_second = 0.95
adam_epsilon = 1e-08
gain_rate = 3.0
matrix_decay = 0.1
norm_epsilon = 1e-06
rope_base = 10000.0

@jax.custom_vjp
def low(v):
    return lax.optimization_barrier(v.astype(jnp.bfloat16)).astype(jnp.float32)

@jax.custom_vjp
def low_back(v):
    return v

def low_keep(v):
    return (low(v), None)

def low_pass(kept, grad):
    return (grad,)

def back_keep(v):
    return (v, None)

def back_low(kept, grad):
    return (low(grad),)
low.defvjp(low_keep, low_pass)
low_back.defvjp(back_keep, back_low)

def matmul(left_side, right_side):
    return jnp.dot(left_side, right_side, precision=lax.Precision.HIGHEST, preferred_element_type=jnp.float32)

def rope_angles(positions):
    half_size = HD // 2
    frequency = rope_base ** (jnp.arange(half_size, dtype=jnp.float32) * (-2.0 / HD))
    angles = positions.astype(jnp.float32)[:, None] * frequency[None, :]
    return (jnp.cos(angles), jnp.sin(angles))

def rotate(vectors, cosine_table, sine_table):
    half_size = vectors.shape[-1] // 2
    first_half = vectors[..., :half_size]
    second_half = vectors[..., half_size:]
    cosine_part = cosine_table[:, None, :]
    sine_part = sine_table[:, None, :]
    return jnp.concatenate([first_half * cosine_part - second_half * sine_part, first_half * sine_part + second_half * cosine_part], axis=-1)

def rms_norm(hidden_rows, gain_row):
    scale_rows = lax.rsqrt(lax.optimization_barrier(jnp.mean(hidden_rows * hidden_rows, axis=-1, keepdims=True)) + norm_epsilon)
    return hidden_rows * scale_rows * gain_row

def slot_index(block_ids, experts_total, capacity):
    count_blocks = block_ids.shape[0]
    flat_ids = block_ids.reshape(count_blocks, -1)
    one_hot = (flat_ids[..., None] == jnp.arange(experts_total, dtype=jnp.int32)).astype(jnp.int32)
    earlier = jnp.cumsum(one_hot, axis=1) - one_hot
    rank_rows = lax.optimization_barrier(jnp.sum(earlier * one_hot, axis=-1))
    block_base = jnp.arange(count_blocks, dtype=jnp.int32)[:, None] * (experts_total * capacity)
    return (block_base + flat_ids * capacity + rank_rows).astype(jnp.int32)

def attend(normed, qkv_matrix, out_matrix, positions):
    length_rows = normed.shape[0]
    projected = matmul(low(normed), qkv_matrix)
    cosine_table, sine_table = rope_angles(positions)
    query_rows = low(rotate(low_back(projected[:, :HQ * HD]).reshape(length_rows, HQ, HD), cosine_table, sine_table))
    key_rows = low(rotate(low_back(projected[:, HQ * HD:(HQ + HK) * HD]).reshape(length_rows, HK, HD), cosine_table, sine_table))
    value_rows = low(low_back(projected[:, (HQ + HK) * HD:])).reshape(length_rows, HK, HD)
    block_rows = min(512, length_rows)
    count_blocks = length_rows // block_rows
    grouped = query_rows.reshape(count_blocks, block_rows, HK, HQ // HK, HD)
    query_pos = positions.reshape(count_blocks, block_rows)

    def one_block(pair):
        block_queries, block_pos = pair
        scores = jnp.einsum('tkgd,skd->kgts', block_queries, key_rows, precision=lax.Precision.HIGHEST) * HD ** (-0.5)
        scores = low_back(scores)
        visible = block_pos[:, None] >= positions[None, :]
        scores = jnp.where(visible, scores, -1e+30)
        top_score = lax.optimization_barrier(jnp.max(scores, axis=-1, keepdims=True))
        exp_scores = jnp.exp(scores - top_score)
        probs_full = exp_scores / lax.optimization_barrier(jnp.sum(exp_scores, axis=-1, keepdims=True))
        mixed_heads = jnp.einsum('kgts,skd->tkgd', low(probs_full), value_rows, precision=lax.Precision.HIGHEST)
        return mixed_heads.reshape(block_rows, HQ * HD)
    heads_out = lax.map(jax.checkpoint(one_block), (grouped, query_pos)).reshape(length_rows, HQ * HD)
    return low_back(matmul(low(low_back(heads_out)), out_matrix))

def experts_apply(normed, in_matrix, down_matrix, ids_rows, gate_rows):
    length_rows = normed.shape[0]
    count_blocks = length_rows // TOK_DEV
    slot_rows = slot_index(ids_rows.reshape(count_blocks, TOK_DEV, TOP), EXPERTS, CAP).reshape(-1)
    sent_rows = low(normed)
    buffer_rows = jnp.zeros((count_blocks * EXPERTS * CAP, D), jnp.float32)
    buffer_rows = buffer_rows.at[slot_rows].set(jnp.repeat(sent_rows, TOP, axis=0))
    per_expert = buffer_rows.reshape(count_blocks, EXPERTS, CAP, D).transpose(1, 0, 2, 3).reshape(EXPERTS, count_blocks * CAP, D)
    both_parts = jnp.einsum('erd,edf->erf', per_expert, in_matrix, precision=lax.Precision.HIGHEST)
    gate_pre = low_back(both_parts[..., :FF])
    up_part = low_back(both_parts[..., FF:])
    hidden_rows = low(jax.nn.gelu(gate_pre, approximate=False) * up_part)
    returned = low(low_back(jnp.einsum('erf,efd->erd', hidden_rows, down_matrix, precision=lax.Precision.HIGHEST)))
    back_rows = returned.reshape(EXPERTS, count_blocks, CAP, D).transpose(1, 0, 2, 3).reshape(-1, D)
    picked = back_rows[slot_rows].reshape(length_rows, TOP, D)
    return lax.optimization_barrier(jnp.sum(gate_rows[..., None] * picked, axis=1))

def run_sequence(params, tokens_seq, ids_seq, gates_seq, positions):
    qkv_all, out_all, in_all, down_all, gain_all = params
    hidden_state = tokens_seq
    for layer_index in range(LAYERS):
        hidden_state = hidden_state + attend(rms_norm(hidden_state, gain_all[layer_index, 0]), qkv_all[layer_index], out_all[layer_index], positions)
        hidden_state = hidden_state + experts_apply(rms_norm(hidden_state, gain_all[layer_index, 1]), in_all[layer_index], down_all[layer_index], ids_seq[layer_index], gates_seq[layer_index])
    return hidden_state

def adam_update(weight, first_moment, second_moment, gradient, step_rate, decay_term):
    first_new = beta_first * first_moment + (1.0 - beta_first) * gradient
    second_new = beta_second * second_moment + (1.0 - beta_second) * gradient * gradient
    first_hat = first_new / (1.0 - beta_first ** STEP)
    second_hat = second_new / (1.0 - beta_second ** STEP)
    weight_new = weight - step_rate * (first_hat / (jnp.sqrt(second_hat) + adam_epsilon) + decay_term * weight)
    return (weight_new, first_new, second_new)

def reference(tokens, cotangent, expert_ids, gate_values, block_order, qkv_weight, qkv_first, qkv_second, out_weight, out_first, out_second, in_weight, in_first, in_second, down_weight, down_first, down_second, norm_gains, gain_first, gain_second):
    positions = (block_order[:, :, None] * TOK_DEV + jnp.arange(TOK_DEV, dtype=jnp.int32)[None, None, :]).reshape(SEQS, LENGTH).astype(jnp.int32)
    ids_seq = jnp.transpose(expert_ids, (1, 0, 2, 3))
    gates_seq = jnp.transpose(gate_values, (1, 0, 2, 3))

    def forward(tokens_all, qkv_all, out_all, in_all, down_all, gain_all):
        params = (low(qkv_all), low(out_all), low(in_all), low(down_all), low(gain_all))

        def one_sequence(carry, pieces):
            tokens_seq, ids_rows, gate_rows, pos_rows = pieces
            return (carry, run_sequence(params, tokens_seq, ids_rows, gate_rows, pos_rows))
        unused, outputs = lax.scan(jax.checkpoint(one_sequence), jnp.zeros((), jnp.float32), (tokens_all, ids_seq, gates_seq, positions))
        return outputs
    output_rows, pull_back = jax.vjp(forward, tokens.astype(jnp.float32), qkv_weight, out_weight, in_weight, down_weight, norm_gains)
    input_grad, qkv_grad, out_grad, in_grad, down_grad, gain_grad = pull_back(cotangent.astype(jnp.float32))
    wide_rate = 5.0 * D ** (-0.5)
    out_rate = 5.0 * (HQ * HD / 16.0) ** (-0.5)
    down_rate = 5.0 * (FF / 4.0) ** (-0.5)
    qkv_new, qkv_first_new, qkv_second_new = adam_update(qkv_weight, qkv_first, qkv_second, qkv_grad, wide_rate, matrix_decay)
    out_new, out_first_new, out_second_new = adam_update(out_weight, out_first, out_second, out_grad, out_rate, matrix_decay)
    in_new, in_first_new, in_second_new = adam_update(in_weight, in_first, in_second, in_grad, wide_rate, matrix_decay)
    down_new, down_first_new, down_second_new = adam_update(down_weight, down_first, down_second, down_grad, down_rate, matrix_decay)
    gains_new, gains_first_new, gains_second_new = adam_update(norm_gains, gain_first, gain_second, gain_grad, gain_rate, 0.0)
    return (output_rows.astype(jnp.bfloat16), input_grad, qkv_new, qkv_first_new, qkv_second_new, out_new, out_first_new, out_second_new, in_new, in_first_new, in_second_new, down_new, down_first_new, down_second_new, gains_new, gains_first_new, gains_second_new)
```

```python
import functools
import itertools
import jax
import jax.numpy as jnp
from jax import lax
from jax.experimental import pallas as pl
from jax.experimental.pallas import tpu as pltpu
from jax.sharding import PartitionSpec as P

D = 1536
HQ = 12
HK = 2
HD = 128
FF = 768
TOP = 4
LAYERS = 2
STEP = 5
EXPERTS = 16
CAP = 40
ROWS = EXPERTS * CAP
QKV = (HQ + 2 * HK) * HD
QW = HQ * HD
KW = HK * HD
YQ = QKV // 4
YO = QW // 4
TOK = 128
KEYS = 1024
GROUP = HQ // HK
GT = GROUP * TOK
score_scale = HD ** (-0.5)
norm_epsilon = 1e-06
BF = jnp.bfloat16
F32 = jnp.float32
MIB = 1 << 20


def dot(a, b, contract):
    return lax.dot_general(a, b, (contract, ((), ())), preferred_element_type=F32)


NN = ((1,), (0,))
NT = ((1,), (1,))
TN = ((0,), (0,))


def split(value):
    high = value.astype(BF)
    return high, (value - high.astype(F32)).astype(BF)


def whole():
    return pl.BlockSpec(memory_space=pltpu.VMEM)


def scalars():
    return pl.BlockSpec(memory_space=pltpu.SMEM)


def anywhere():
    return pl.BlockSpec(memory_space=pl.ANY)


def call(body, outs, ins, specs, scratch, flops, moved, name, mib=40, out_specs=None, grid=None):
    return pl.pallas_call(
        body,
        out_shape=[jax.ShapeDtypeStruct(s, t) for s, t in outs],
        in_specs=specs,
        out_specs=out_specs or [whole() for _ in outs],
        scratch_shapes=scratch,
        grid=grid or (),
        compiler_params=pltpu.CompilerParams(vmem_limit_bytes=mib * MIB),
        cost_estimate=pl.CostEstimate(flops=int(flops), bytes_accessed=int(moved), transcendentals=0),
        name=name,
    )(*ins)


def turn(head, cosine, sine):
    return head * cosine + pltpu.roll(head, HD // 2, 1) * sine


def rope_heads(part, y, cosine, sine):
    heads = []
    for i in range(4):
        head = part[:, i * HD : (i + 1) * HD]
        heads.append(head if y == 3 and i >= 2 else turn(head, cosine, sine))
    return jnp.concatenate(heads, axis=1)


def load_parts(w_ref, buf, sem, column, width):
    copies = [
        pltpu.make_async_copy(w_ref.at[:, y, :, pl.ds(column, width)], buf.at[y], sem.at[y])
        for y in range(4)
    ]
    for copy in copies:
        copy.start()
    return copies


def project_body(add, *refs):
    if add:
        (base, came, high, low, gain, cosine, sine, w, hidden, attn_in, scale, out, buf, sem) = refs
    else:
        (base, gain, cosine, sine, w, attn_in, scale, out, buf, sem) = refs
    copies = load_parts(w, buf, sem, 0, YQ)
    h = base[...].astype(F32)
    if add:
        rows = came[...]
        h = h + (dot(high[...], rows, NN) + dot(low[...], rows, NN))
        hidden[...] = h
    factor = lax.rsqrt(jnp.mean(h * h, axis=1, keepdims=True) + norm_epsilon)
    scale[...] = factor
    fed = (h * factor * gain[...]).astype(BF)
    attn_in[...] = fed
    for y in range(4):
        copies[y].wait()
        part = dot(fed, buf[y].reshape(D, YQ), NN)
        out[:, y * YQ : (y + 1) * YQ] = rope_heads(part, y, cosine[...], sine[...]).astype(BF)


def project(base, gain, cosine, sine, w, extra=None):
    ins = [base] + list(extra or ()) + [gain, cosine, sine, w]
    outs = [((TOK, D), BF), ((TOK, 1), F32), ((TOK, QKV), BF)]
    if extra:
        outs = [((TOK, D), F32)] + outs
    return call(
        functools.partial(project_body, bool(extra)),
        outs,
        ins,
        [whole() for _ in ins[:-1]] + [anywhere()],
        [pltpu.VMEM((4, 32, 48, YQ), BF), pltpu.SemaphoreType.DMA((4,))],
        2 * TOK * D * QKV,
        2 * D * QKV + 8 * TOK * D,
        "project",
    )


def keep_keys(kv_refs, buf):
    for k, ref in enumerate(kv_refs):
        for h in range(2):
            buf[(2 * k + h) * TOK : (2 * k + h + 1) * TOK, :] = ref[h]


def stack_heads(ref, j):
    return jnp.concatenate(
        [ref[:, (j * GROUP + i) * HD : (j * GROUP + i + 1) * HD] for i in range(GROUP)], axis=0
    )


def unstack(total):
    return jnp.concatenate(
        [total[:, i * TOK : (i + 1) * TOK].T for i in range(GROUP)], axis=1
    )


def attend_body(qkv, kv0, kv1, kv2, kv3, key_pos, query_pos, mixed, norm, buf, keep):
    keep_keys((kv0, kv1, kv2, kv3), buf)
    places = jnp.concatenate([query_pos[...]] * GROUP, axis=1)
    for j in range(HK):
        queries = stack_heads(qkv, j)

        def score(b, top):
            at = pl.ds(pl.multiple_of(b * TOK, TOK), TOK)
            keys = buf[at, j * HD : (j + 1) * HD]
            values = dot(keys, queries, NT) * score_scale
            values = jnp.where(key_pos[at, :] <= places, values, -1e30)
            keep[at, :] = values
            return jnp.maximum(top, jnp.max(values, axis=0, keepdims=True))

        top = lax.fori_loop(0, KEYS // TOK, score, jnp.full((1, GT), -1e30, F32))

        def mix(b, carry):
            total, share = carry
            at = pl.ds(pl.multiple_of(b * TOK, TOK), TOK)
            e = jnp.exp(keep[at, :] - top)
            values = buf[at, KW + j * HD : KW + (j + 1) * HD]
            share = share + jnp.sum(e, axis=0, keepdims=True)
            return total + dot(values, e.astype(BF), TN), share

        total, share = lax.fori_loop(
            0, KEYS // TOK, mix, (jnp.zeros((HD, GT), F32), jnp.zeros((1, GT), F32))
        )
        norm[j : j + 1, :] = top + jnp.log(share)
        mixed[:, j * GT : (j + 1) * GT] = unstack(total / share).astype(BF)


def attend(qkv, kv, key_pos, query_pos):
    ins = [qkv, *kv, key_pos, query_pos]
    return call(
        attend_body,
        [((TOK, QW), BF), ((HK, GT), F32)],
        ins,
        [whole() for _ in ins],
        [pltpu.VMEM((KEYS, 2 * KW), BF), pltpu.VMEM((KEYS, GT), F32)],
        4 * TOK * KEYS * QW,
        2 * KEYS * 2 * KW,
        "attend",
    )


def attend_back_body(
    qkv, kv0, kv1, kv2, kv3, key_pos, query_pos, norm, d_mixed, d_queries, d_pairs, buf, kept, given
):
    keep_keys((kv0, kv1, kv2, kv3), buf)
    places = jnp.concatenate([query_pos[...]] * GROUP, axis=1)
    for j in range(HK):
        queries = stack_heads(qkv, j)
        upstream = stack_heads(d_mixed, j)
        level = norm[j : j + 1, :]

        def probs(b, delta):
            at = pl.ds(pl.multiple_of(b * TOK, TOK), TOK)
            keys = buf[at, j * HD : (j + 1) * HD]
            values = buf[at, KW + j * HD : KW + (j + 1) * HD]
            scores = dot(keys, queries, NT) * score_scale
            p = jnp.where(key_pos[at, :] <= places, jnp.exp(scores - level), 0.0)
            dp = dot(values, upstream, NT)
            kept[at, :] = p
            given[at, :] = dp
            d_pairs[at, KW + j * HD : KW + (j + 1) * HD] = dot(p.astype(BF), upstream, NN).astype(BF)
            return delta + jnp.sum(p * dp, axis=0, keepdims=True)

        delta = lax.fori_loop(0, KEYS // TOK, probs, jnp.zeros((1, GT), F32))

        def back(b, total):
            at = pl.ds(pl.multiple_of(b * TOK, TOK), TOK)
            keys = buf[at, j * HD : (j + 1) * HD]
            ds = (kept[at, :] * (given[at, :] - delta)).astype(BF)
            d_pairs[at, j * HD : (j + 1) * HD] = (dot(ds, queries, NN) * score_scale).astype(BF)
            return total + dot(keys, ds, TN)

        total = lax.fori_loop(0, KEYS // TOK, back, jnp.zeros((HD, GT), F32))
        d_queries[:, j * GT : (j + 1) * GT] = unstack(total * score_scale)


def attend_back(qkv, kv, key_pos, query_pos, norm, d_mixed):
    ins = [qkv, *kv, key_pos, query_pos, norm, d_mixed]
    return call(
        attend_back_body,
        [((TOK, QW), F32), ((KEYS, 2 * KW), BF)],
        ins,
        [whole() for _ in ins],
        [pltpu.VMEM((KEYS, 2 * KW), BF), pltpu.VMEM((KEYS, GT), F32), pltpu.VMEM((KEYS, GT), F32)],
        10 * TOK * KEYS * QW,
        4 * KEYS * 2 * KW,
        "attend_back",
    )


def branch_body(base, mixed, gain, pick, w, hidden, scale, sent, buf, sem):
    copies = load_parts(w, buf, sem, YQ, YO)
    total = base[...].astype(F32)
    for y in range(4):
        copies[y].wait()
        total = total + dot(mixed[:, y * YO : (y + 1) * YO], buf[y].reshape(D, YO), NT)
    hidden[...] = total
    factor = lax.rsqrt(jnp.mean(total * total, axis=1, keepdims=True) + norm_epsilon)
    scale[...] = factor
    fed = (total * factor * gain[...]).astype(BF)
    sent[...] = dot(pick[...], fed, NN).astype(BF)


def branch(base, mixed, gain, pick, w):
    ins = [base, mixed, gain, pick, w]
    return call(
        branch_body,
        [((TOK, D), F32), ((TOK, 1), F32), ((ROWS, D), BF)],
        ins,
        [whole() for _ in ins[:-1]] + [anywhere()],
        [pltpu.VMEM((4, 32, 48, YO), BF), pltpu.SemaphoreType.DMA((4,))],
        2 * TOK * D * QW + 2 * TOK * D * ROWS,
        2 * D * QW + 2 * ROWS * D,
        "branch",
    )


BLOCK = 320


def load_expert(w_refs, places, buf, sem):
    copies = []
    for ref in w_refs:
        lead = ref.shape[:-2]
        for at in itertools.product(*[range(n) for n in lead]):
            row = pl.multiple_of(places[len(copies)] * 96, 96)
            copies.append(
                pltpu.make_async_copy(
                    ref.at[at] if at else ref, buf.at[pl.ds(row, 96), :], sem.at[len(copies)]
                )
            )
    for copy in copies:
        copy.start()
    for copy in copies:
        copy.wait()


def gelu_parts(x):
    cdf = 0.5 * (1.0 + lax.erf(x * (0.5**0.5)))
    density = jnp.exp(-0.5 * x * x) * 0.3989422804014327
    return x * cdf, cdf + x * density


def ffn_body(n, places, received, *refs):
    w_refs, (returned, hidden, act, slope, buf, sem) = refs[:n], refs[n:]

    @pl.when(pl.program_id(0) == 0)
    def _():
        load_expert(w_refs, places, buf, sem)

    both = dot(received[...], buf[:, : 2 * FF], NN)
    up = both[:, FF:]
    gelu, gelu_slope = gelu_parts(both[:, :FF])
    low = (gelu * up).astype(BF)
    hidden[...] = low
    act[...] = gelu
    slope[...] = gelu_slope * up
    returned[...] = dot(low, buf[:, 2 * FF :], NT).astype(BF)


def row_block(width):
    return pl.BlockSpec((BLOCK, width), lambda i: (i, 0))


def ffn(received, w_list, places):
    return call(
        functools.partial(ffn_body, len(w_list)),
        [((ROWS, D), BF), ((ROWS, FF), BF), ((ROWS, FF), F32), ((ROWS, FF), F32)],
        [places, received, *w_list],
        [scalars(), row_block(D)] + [anywhere() for _ in w_list],
        [pltpu.VMEM((D, 3 * FF), BF), pltpu.SemaphoreType.DMA((16,))],
        2 * ROWS * D * 3 * FF,
        2 * D * 3 * FF + 16 * ROWS * FF,
        "ffn",
        out_specs=[row_block(D), row_block(FF), row_block(FF), row_block(FF)],
        grid=(ROWS // BLOCK,),
    )


def ffn_back_body(n, places, owner, act, slope, *refs):
    w_refs, (d_rows, d_both, buf, sem) = refs[:n], refs[n:]

    @pl.when(pl.program_id(0) == 0)
    def _():
        load_expert(w_refs, places, buf, sem)

    d_hidden = dot(owner[...], buf[:, 2 * FF :], NN)
    both = jnp.concatenate([d_hidden * slope[...], d_hidden * act[...]], axis=1).astype(BF)
    d_both[...] = both
    d_rows[...] = dot(both, buf[:, : 2 * FF], NT).astype(BF)


def ffn_back(owner, act, slope, w_list, places):
    return call(
        functools.partial(ffn_back_body, len(w_list)),
        [((ROWS, D), BF), ((ROWS, 2 * FF), BF)],
        [places, owner, act, slope, *w_list],
        [scalars(), row_block(D), row_block(FF), row_block(FF)] + [anywhere() for _ in w_list],
        [pltpu.VMEM((D, 3 * FF), BF), pltpu.SemaphoreType.DMA((16,))],
        2 * ROWS * D * 3 * FF,
        2 * D * 3 * FF + 16 * ROWS * FF,
        "ffn_back",
        out_specs=[row_block(D), row_block(2 * FF)],
        grid=(ROWS // BLOCK,),
    )


def ffn_grad_body(received, d_both, owner, hidden, out):
    out[:, 0, :, : 2 * FF] = dot(received[...], d_both[...], TN).astype(BF).reshape(8, 96, 2 * FF)
    out[:, 0, :, 2 * FF :] = dot(owner[...], hidden[...], TN).astype(BF).reshape(8, 96, FF)


def ffn_grad(received, d_both, owner, hidden):
    half = pl.BlockSpec((ROWS, D // 2), lambda i: (0, i))
    fixed = lambda width: pl.BlockSpec((ROWS, width), lambda i: (0, 0))
    return call(
        ffn_grad_body,
        [((8, 2, 96, 3 * FF), BF)],
        [received, d_both, owner, hidden],
        [half, fixed(2 * FF), half, fixed(FF)],
        [],
        2 * ROWS * D * 3 * FF,
        2 * D * 3 * FF + 8 * ROWS * D,
        "ffn_grad",
        out_specs=[pl.BlockSpec((8, 1, 96, 3 * FF), lambda i: (0, i, 0, 0))],
        grid=(2,),
    )[0]


def norm_back(upstream, rows, factor, gain):
    normed = rows * factor
    scaled = upstream * gain
    return (
        factor * (scaled - normed * jnp.mean(scaled * normed, axis=1, keepdims=True)),
        jnp.sum(upstream * normed, axis=0, keepdims=True),
    )


def branch_back_body(source, pick_t, base, scale, gain, d_out, w, d_base, low, d_mixed, d_gain, buf, sem):
    copies = load_parts(w, buf, sem, YQ, YO)
    d_fed = dot(pick_t[...], source[...], NN)
    term, d_gain[...] = norm_back(d_fed, base[...], scale[...], gain[...])
    total = d_out[...].astype(F32) + term
    d_base[...] = total
    rounded = total.astype(BF)
    low[...] = rounded
    for y in range(4):
        copies[y].wait()
        d_mixed[:, y * YO : (y + 1) * YO] = dot(rounded, buf[y].reshape(D, YO), NN).astype(BF)


def branch_back(source, pick_t, base, scale, gain, d_out, w):
    ins = [source, pick_t, base, scale, gain, d_out, w]
    return call(
        branch_back_body,
        [((TOK, D), F32), ((TOK, D), BF), ((TOK, QW), BF), ((1, D), F32)],
        ins,
        [whole() for _ in ins[:-1]] + [anywhere()],
        [pltpu.VMEM((4, 32, 48, YO), BF), pltpu.SemaphoreType.DMA((4,))],
        2 * TOK * D * QW + 2 * TOK * D * ROWS,
        2 * D * QW + 2 * ROWS * D,
        "branch_back",
    )


def project_back_body(last, *refs):
    if last:
        (dq, dkv, cosine, sine, base, scale, gain, d_out, w, d_base, d_proj, d_gain, buf, sem) = refs
    else:
        (dq, dkv, cosine, sine, base, scale, gain, d_out, pick, gate, w) = refs[:11]
        (d_base, d_proj, d_gain, sent, buf, sem) = refs[11:]
    copies = load_parts(w, buf, sem, 0, YQ)
    total = jnp.zeros((TOK, D), F32)
    for y in range(4):
        part = dq[:, y * YQ : (y + 1) * YQ] if y < 3 else dkv[...]
        rounded = rope_heads(part, y, cosine[...], -sine[...]).astype(BF)
        d_proj[:, y * YQ : (y + 1) * YQ] = rounded
        copies[y].wait()
        total = total + dot(rounded, buf[y].reshape(D, YQ), NT)
    term, d_gain[...] = norm_back(total, base[...].astype(F32), scale[...], gain[...])
    d_hidden = d_out[...] + term
    d_base[...] = d_hidden
    if not last:
        high, low = split(d_hidden)
        rows = dot(pick[...], high, NN) + dot(pick[...], low, NN)
        sent[...] = (rows * gate[...]).astype(BF)


def project_back(dq, dkv, cosine, sine, base, scale, gain, d_out, w, extra=None):
    ins = [dq, dkv, cosine, sine, base, scale, gain, d_out] + list(extra or ()) + [w]
    outs = [((TOK, D), F32), ((TOK, QKV), BF), ((1, D), F32)]
    if extra:
        outs = outs + [((ROWS, D), BF)]
    return call(
        functools.partial(project_back_body, not extra),
        outs,
        ins,
        [whole() for _ in ins[:-1]] + [anywhere()],
        [pltpu.VMEM((4, 32, 48, YQ), BF), pltpu.SemaphoreType.DMA((4,))],
        2 * TOK * D * QKV,
        2 * D * QKV + 8 * TOK * D,
        "project_back",
    )


def wide_grad_body(core, one, two, three, four, out):
    del core
    out[0, 0, :, :YQ] = dot(one[...], two[...], TN).astype(BF)
    out[0, 0, :, YQ:] = dot(three[...], four[...], TN).astype(BF)


def half_of(rows):
    return pl.BlockSpec((rows, D // 2), lambda i, y, core: (0, (i + core[0]) % 2))


def wide_grad(core, attn_in, d_projected, d_branch, mixed):
    return pl.pallas_call(
        wide_grad_body,
        out_shape=jax.ShapeDtypeStruct((2, 4, D // 2, YQ + YO), BF),
        grid_spec=pltpu.PrefetchScalarGridSpec(
            num_scalar_prefetch=1,
            grid=(2, 4),
            in_specs=[
                half_of(TOK),
                pl.BlockSpec((TOK, YQ), lambda i, y, core: (0, y)),
                half_of(TOK),
                pl.BlockSpec((TOK, YO), lambda i, y, core: (0, y)),
            ],
            out_specs=pl.BlockSpec((1, 1, D // 2, YQ + YO), lambda i, y, core: (i, y, 0, 0)),
        ),
        compiler_params=pltpu.CompilerParams(vmem_limit_bytes=40 * MIB),
        cost_estimate=pl.CostEstimate(
            flops=2 * TOK * D * (QKV + QW), bytes_accessed=2 * D * (QKV + QW), transcendentals=0
        ),
        name="wide_grad",
    )(core, attn_in, d_projected, d_branch, mixed)


def spread_matrices():
    row = jnp.arange(384, dtype=jnp.int32)[:, None]
    column = jnp.arange(768, dtype=jnp.int32)[None, :]
    place = (column // 24) * 12 + column % 12
    late = (column % 24) // 12
    return jnp.stack([((row == place) & (late == h)).astype(BF) for h in range(2)])


def owner_grad_body(core, left, right, spread, out):
    del core
    width = right.shape[1] // 2
    rows = left[...]
    both = jnp.concatenate([dot(rows, spread[h], NN).astype(BF) for h in range(2)], axis=0)
    sides = jnp.concatenate([right[:, :width], right[:, width:]], axis=0)
    out[0] = dot(both, sides, TN).astype(BF).reshape(32, 24, width)


def owner_grad(core, left, right, spread):
    width = right.shape[1] // 2
    return pl.pallas_call(
        owner_grad_body,
        out_shape=jax.ShapeDtypeStruct((2, 64, 24, width), BF),
        grid_spec=pltpu.PrefetchScalarGridSpec(
            num_scalar_prefetch=1,
            grid=(2, 2),
            in_specs=[
                pl.BlockSpec((TOK, 384), lambda i, s, core: (0, ((i + core[0]) % 2) * 2 + s)),
                pl.BlockSpec((TOK, 2 * width), lambda i, s, core: (0, 0)),
                pl.BlockSpec((2, 384, 768), lambda i, s, core: (0, 0, 0)),
            ],
            out_specs=pl.BlockSpec((1, 32, 24, width), lambda i, s, core: (i, s, 0, 0)),
        ),
        compiler_params=pltpu.CompilerParams(vmem_limit_bytes=40 * MIB),
        cost_estimate=pl.CostEstimate(
            flops=4 * TOK * D * 2 * width, bytes_accessed=4 * D * width, transcendentals=0
        ),
        name="owner_grad",
    )(core, left, right, spread)


beta_first = 0.9
beta_second = 0.95
adam_epsilon = 1e-08
gain_rate = 3.0
matrix_decay = 0.1
rope_base = 10000.0
ALL = ("dp", "context", "experts")
OWNERS = ("dp", "experts")
LINE = ("context", "experts")
Y_GROUPS = [[0, 1, 2, 3], [4, 5, 6, 7]]


def send_z(value, hop):
    pairs = [(z * 2 + h, ((z + hop) % 4) * 2 + h) for z in range(4) for h in range(2)]
    return lax.ppermute(value, "context", pairs)


def swap_xh(value):
    pairs = [(z * 2 + h, z * 2 + 1 - h) for z in range(4) for h in range(2)]
    return lax.ppermute(value, "context", pairs)


def send_y(value, hop):
    pairs = [(l * 4 + y, l * 4 + (y + hop) % 4) for l in range(2) for y in range(4)]
    return lax.ppermute(value, "experts", pairs)


def swap_xl(value):
    pairs = [(l * 4 + y, (1 - l) * 4 + y) for l in range(2) for y in range(4)]
    return lax.ppermute(value, "experts", pairs)


def swap_core(value):
    return lax.ppermute(value, "dp", [(0, 1), (1, 0)])


def place():
    context = lax.axis_index("context")
    experts = lax.axis_index("experts")
    return dict(d=lax.axis_index("dp"), z=context // 2, xh=context % 2, xl=experts // 4, y=experts % 4)


def ordered(flag, own, other):
    return jnp.where(flag == 0, jnp.stack([own, other]), jnp.stack([other, own]))


def keep_and_give(pair, flag):
    return (
        lax.dynamic_index_in_dim(pair, flag, 0, False),
        lax.dynamic_index_in_dim(pair, 1 - flag, 0, False),
    )


def rope_tables(positions):
    frequency = rope_base ** (jnp.arange(HD // 2, dtype=F32) * (-2.0 / HD))
    angles = positions.astype(F32)[:, None] * frequency[None, :]
    cosine, sine = jnp.cos(angles), jnp.sin(angles)
    return jnp.concatenate([cosine, cosine], axis=1), jnp.concatenate([-sine, sine], axis=1)


def adam_update(weight, first_moment, second_moment, gradient, step_rate, decay_term):
    first_new = beta_first * first_moment + (1.0 - beta_first) * gradient
    second_new = beta_second * second_moment + (1.0 - beta_second) * gradient * gradient
    first_hat = first_new / (1.0 - beta_first**STEP)
    second_hat = second_new / (1.0 - beta_second**STEP)
    weight_new = weight - step_rate * (
        first_hat / (jnp.sqrt(second_hat) + adam_epsilon) + decay_term * weight
    )
    return (weight_new, first_new, second_new)


def routing(ids, gates):
    flat = ids.reshape(-1)
    one_hot = (flat[:, None] == jnp.arange(EXPERTS, dtype=jnp.int32)).astype(jnp.int32)
    earlier = jnp.cumsum(one_hot, axis=0) - one_hot
    rank = jnp.sum(earlier * one_hot, axis=-1)
    owner = (flat % 2) * (EXPERTS // 2) + flat // 2
    slots = (owner * CAP + rank).reshape(ids.shape)
    hit = slots[:, :, None] == jnp.arange(ROWS, dtype=jnp.int32)
    pick = jnp.any(hit, axis=1).astype(BF)
    weight = jnp.sum(jnp.where(hit, gates[:, :, None], 0.0), axis=1)
    slot_gate = jnp.sum(weight, axis=0)[:, None]
    weight_high, weight_low = split(weight)
    return pick, pick.T, weight_high, weight_low, slot_gate


def exchange(rows):
    return lax.all_to_all(
        rows.reshape(EXPERTS, CAP, D), OWNERS, split_axis=0, concat_axis=0, tiled=True
    ).reshape(ROWS, D)


def gather_keys(rows):
    pair = ordered(place()["xh"], rows, swap_xh(rows))
    return [pair] + [send_z(pair, k) for k in (1, 2, 3)]


def return_keys(grads):
    total = grads[0].astype(F32)
    for k in (1, 2, 3):
        total = total + send_z(grads[k], -k).astype(F32)
    own, other = keep_and_give(total, place()["xh"])
    return own + swap_xh(other.astype(BF)).astype(F32)


def column_blocks(qkv_weight, out_weight):
    return jnp.concatenate(
        [
            qkv_weight.astype(BF).reshape(LAYERS, -1, 4, YQ),
            out_weight.astype(BF).transpose(0, 2, 1).reshape(LAYERS, -1, 4, YO),
        ],
        axis=-1,
    ).transpose(2, 0, 1, 3)


def core_pair(in_weight, down_weight):
    both = jnp.concatenate(
        [in_weight.astype(BF), down_weight.astype(BF).transpose(0, 2, 1)], axis=-1
    )
    own, give = keep_and_give(both, lax.axis_index("dp"))
    return own, swap_core(give)


def scatter_wide(grads):
    at = place()
    width = YQ + YO
    half = (grads[0].astype(F32) + swap_core(grads[1]).astype(F32)).astype(BF)
    total = lax.dynamic_index_in_dim(half, at["y"], 0, False).astype(F32)
    for k in (1, 2, 3):
        chunk = lax.dynamic_index_in_dim(half, (at["y"] + k) % 4, 0, False)
        total = total + send_y(chunk, k).astype(F32)
    part = total.astype(BF).reshape(4, 192, width)
    total = lax.dynamic_index_in_dim(part, at["z"], 0, False).astype(F32)
    for k in (1, 2, 3):
        chunk = lax.dynamic_index_in_dim(part, (at["z"] + k) % 4, 0, False)
        total = total + send_z(chunk, k).astype(F32)
    for flag, swap, rows in ((at["xh"], swap_xh, 96), (at["xl"], swap_xl, 48)):
        kept, other = keep_and_give(total.reshape(2, rows, width), flag)
        total = kept + swap(other.astype(BF)).astype(F32)
    last = lax.all_to_all(
        total.astype(BF).reshape(4, 12, width),
        "experts",
        0,
        0,
        axis_index_groups=Y_GROUPS,
        tiled=True,
    )
    last = last.astype(F32).transpose(1, 0, 2)
    return last[:, :, :YQ].reshape(12, QKV), last[:, :, YQ:].reshape(12, QW)


def scatter_owner(grads):
    half = (grads[0].astype(F32) + swap_core(grads[1]).astype(F32)).astype(BF)
    parts = lax.all_to_all(half, LINE, 0, 0, tiled=True)
    total = jnp.sum(parts.astype(F32), axis=0)
    return jnp.concatenate([total[:12], total[12:]], axis=1)


def scatter_experts(grads):
    pair = lax.psum_scatter(grads, "context", scatter_dimension=0)
    core = lax.axis_index("dp")
    own, give = keep_and_give(pair, core)
    return ordered(core, own, swap_core(give)).astype(F32)


def spread_gains(rows):
    return rows.reshape(4, 128, 12).transpose(1, 0, 2).reshape(128, 1, 48)


def local(
    tokens,
    cotangent,
    expert_ids,
    gate_values,
    block_order,
    qkv_weight,
    qkv_first,
    qkv_second,
    out_weight,
    out_first,
    out_second,
    in_weight,
    in_first,
    in_second,
    down_weight,
    down_first,
    down_second,
    norm_gains,
    gain_first,
    gain_second,
):
    at = place()
    core = at["d"].astype(jnp.int32).reshape(1)
    blocks = lax.all_to_all(
        column_blocks(qkv_weight, out_weight),
        "experts",
        0,
        0,
        axis_index_groups=Y_GROUPS,
        tiled=True,
    ).transpose(1, 0, 2, 3)
    projections = [
        lax.all_gather(blocks[l].reshape(48, YQ + YO), ALL, axis=0).reshape(32, 4, 48, YQ + YO)
        for l in range(LAYERS)
    ]
    gain_rows = norm_gains.astype(BF).astype(F32).reshape(1, 1, 48)
    gains = lax.all_to_all(jnp.broadcast_to(gain_rows, (128, 1, 48)), ALL, 0, 0, tiled=True)
    gains = gains.reshape(128, 4, 12).transpose(1, 0, 2).reshape(4, 1, D)

    own, other = core_pair(in_weight[0], down_weight[0])
    column = [own] + [send_z(own, k) for k in (1, 2, 3)]
    beside = [swap_xh(rows) for rows in column]
    pair = ordered(at["xh"], other, swap_xh(other))
    pairs = [pair] + [send_z(pair, k) for k in (1, 2, 3)]
    turns = (at["z"] - jnp.arange(4, dtype=jnp.int32)) % 4
    both = jnp.arange(2, dtype=jnp.int32)
    direct_places = jnp.concatenate(
        [
            at["d"] * 8 + turns * 2 + at["xh"],
            at["d"] * 8 + turns * 2 + 1 - at["xh"],
            ((1 - at["d"]) * 8 + turns[:, None] * 2 + both[None, :]).reshape(-1),
        ]
    ).astype(jnp.int32)
    gathered_places = (
        jnp.arange(8, dtype=jnp.int32)[:, None] + 8 * both[None, :]
    ).reshape(-1)
    later = ordered(at["d"], *core_pair(in_weight[1], down_weight[1]))
    experts = [
        (column + beside + pairs, direct_places),
        ([lax.all_gather(later, "context", axis=0)], gathered_places),
    ]

    order_row = block_order[0]
    offsets = jnp.arange(TOK, dtype=jnp.int32)
    places = jnp.arange(8, dtype=jnp.int32)
    source = (turns[:, None] * 2 + both[None, :]).reshape(-1)
    key_block = jnp.sum(jnp.where(source[:, None] == places, order_row, 0), axis=1)
    own_block = jnp.sum(jnp.where(places == lax.axis_index("context"), order_row, 0))
    query_pos = own_block * TOK + offsets
    key_pos = (key_block[:, None] * TOK + offsets[None, :]).reshape(-1, 1)
    cosine, sine = rope_tables(query_pos)
    query_pos = query_pos.reshape(1, -1)
    routes = [routing(expert_ids[l, 0], gate_values[l, 0]) for l in range(LAYERS)]
    spread = spread_matrices()

    saved = []
    base, came_back = tokens[0], None
    for l in range(LAYERS):
        pick, pick_t, weight_high, weight_low, slot_gate = routes[l]
        if l == 0:
            attn_in, scale_one, qkv = project(base, gains[0], cosine, sine, projections[0])
        else:
            base, attn_in, scale_one, qkv = project(
                base, gains[2 * l], cosine, sine, projections[l], came_back
            )
        kv = gather_keys(qkv[:, QW:])
        mixed, level = attend(qkv, kv, key_pos, query_pos)
        middle, scale_two, sent = branch(base, mixed, gains[2 * l + 1], pick_t, projections[l])
        received = exchange(sent)
        weights, chunk_places = experts[l]
        returned, hidden, act, slope = ffn(received, weights, chunk_places)
        came_back = (exchange(returned), weight_high, weight_low)
        saved.append(
            (base, attn_in, scale_one, qkv, kv, mixed, level, middle, scale_two, received, hidden, act, slope)
        )
        base = middle
    result = middle + (
        dot(came_back[1], came_back[0], NN) + dot(came_back[2], came_back[0], NN)
    )

    d_out = cotangent[0]
    pick_t, slot_gate = routes[-1][1], routes[-1][4]
    sent = (dot(pick_t, d_out, NN) * slot_gate).astype(BF)
    projection_sums = [None] * LAYERS
    expert_sums = [None] * LAYERS
    gain_grads = [None] * (2 * LAYERS)
    for l in reversed(range(LAYERS)):
        (base, attn_in, scale_one, qkv, kv, mixed, level, middle, scale_two, received, hidden, act, slope) = (
            saved[l]
        )
        weights, chunk_places = experts[l]
        owner = exchange(sent)
        d_rows, d_both = ffn_back(owner, act, slope, weights, chunk_places)
        came_grad = exchange(d_rows)
        expert_grad = ffn_grad(received, d_both, owner, hidden)
        if l < LAYERS - 1:
            expert_grad, expert_sums[l + 1] = lax.optimization_barrier(
                (expert_grad, expert_sums[l + 1])
            )
        expert_sums[l] = scatter_experts(expert_grad)
        d_base, d_branch, d_mixed, gain_grads[2 * l + 1] = branch_back(
            came_grad, routes[l][0], middle, scale_two, gains[2 * l + 1], d_out, projections[l]
        )
        if l == 0:
            out_rows = scatter_owner(owner_grad(core, d_branch, mixed, spread))
        d_queries, d_pairs = attend_back(qkv, kv, key_pos, query_pos, level, d_mixed)
        d_key_value = return_keys(d_pairs.reshape(4, 2, TOK, 2 * KW))
        extra = (routes[l - 1][1], routes[l - 1][4]) if l else None
        back = project_back(
            d_queries,
            d_key_value,
            cosine,
            sine,
            base,
            scale_one,
            gains[2 * l],
            d_base,
            projections[l],
            extra,
        )
        d_out, d_projected, gain_grads[2 * l] = back[:3]
        if l:
            sent = back[3]
            projection_sums[l] = scatter_wide(
                wide_grad(core, attn_in, d_projected, d_branch, mixed)
            )
        else:
            projection_sums[l] = (
                scatter_owner(owner_grad(core, attn_in, d_projected, spread)),
                out_rows,
            )
    gain_sum = lax.all_to_all(
        spread_gains(jnp.concatenate(gain_grads, axis=0)), ALL, 0, 0, tiled=True
    )
    gain_sum = jnp.sum(gain_sum, axis=0).reshape(2, 2, 12)
    qkv_sum = jnp.stack([s[0] for s in projection_sums])
    out_sum = jnp.stack([s[1] for s in projection_sums]).transpose(0, 2, 1)
    in_sum = jnp.stack([s[:, :, : 2 * FF] for s in expert_sums])
    down_sum = jnp.stack([s[:, :, 2 * FF :] for s in expert_sums]).transpose(0, 1, 3, 2)
    wide_rate = 5.0 * D ** (-0.5)
    out_rate = 5.0 * (HQ * HD / 16.0) ** (-0.5)
    down_rate = 5.0 * (FF / 4.0) ** (-0.5)
    updates = (
        adam_update(qkv_weight, qkv_first, qkv_second, qkv_sum, wide_rate, matrix_decay)
        + adam_update(out_weight, out_first, out_second, out_sum, out_rate, matrix_decay)
        + adam_update(in_weight, in_first, in_second, in_sum, wide_rate, matrix_decay)
        + adam_update(down_weight, down_first, down_second, down_sum, down_rate, matrix_decay)
        + adam_update(norm_gains, gain_first, gain_second, gain_sum, gain_rate, 0.0)
    )
    return (result.astype(BF)[None], d_out[None]) + updates


def solution(mesh):
    rows = P(("dp", "experts"), "context", None)
    routes = P(None, ("dp", "experts"), "context", None)
    qkv = P(None, ALL, None)
    out = P(None, None, ALL)
    wide = P(None, "experts", ("dp", "context"), None)
    down = P(None, "experts", None, ("dp", "context"))
    states = (qkv,) * 3 + (out,) * 3 + (wide,) * 3 + (down,) * 3 + (out,) * 3
    return jax.shard_map(
        local,
        mesh=mesh,
        in_specs=(rows, rows, routes, routes, P(("dp", "experts"), None)) + states,
        out_specs=(rows, rows) + states,
        check_vma=False,
    )
```

```python
import functools
import itertools
import jax
import jax.numpy as jnp
from jax import lax
from jax.experimental import pallas as pl
from jax.experimental.pallas import tpu as pltpu
from jax.sharding import PartitionSpec as P

D = 1536
HQ = 12
HK = 2
HD = 128
FF = 768
TOP = 4
LAYERS = 2
STEP = 5
EXPERTS = 16
CAP = 40
ROWS = EXPERTS * CAP
QKV = (HQ + 2 * HK) * HD
QW = HQ * HD
KW = HK * HD
YQ = QKV // 4
YO = QW // 4
TOK = 128
KEYS = 1024
GROUP = HQ // HK
GT = GROUP * TOK
score_scale = HD ** (-0.5)
norm_epsilon = 1e-06
BF = jnp.bfloat16
F32 = jnp.float32
MIB = 1 << 20


def dot(a, b, contract):
    return lax.dot_general(a, b, (contract, ((), ())), preferred_element_type=F32)


NN = ((1,), (0,))
NT = ((1,), (1,))
TN = ((0,), (0,))


def split(value):
    high = value.astype(BF)
    return high, (value - high.astype(F32)).astype(BF)


def whole():
    return pl.BlockSpec(memory_space=pltpu.VMEM)


def scalars():
    return pl.BlockSpec(memory_space=pltpu.SMEM)


def anywhere():
    return pl.BlockSpec(memory_space=pltpu.HBM)


def call(body, outs, ins, specs, scratch, flops, moved, name, mib=40, out_specs=None, grid=None):
    return pl.pallas_call(
        body,
        out_shape=[jax.ShapeDtypeStruct(s, t) for s, t in outs],
        in_specs=specs,
        out_specs=out_specs or [whole() for _ in outs],
        scratch_shapes=scratch,
        grid=grid or (),
        compiler_params=pltpu.CompilerParams(vmem_limit_bytes=mib * MIB),
        cost_estimate=pl.CostEstimate(flops=int(flops), bytes_accessed=int(moved), transcendentals=0),
        name=name,
    )(*ins)


def turn(head, cosine, sine):
    return head * cosine + pltpu.roll(head, HD // 2, 1) * sine


def rope_heads(part, y, cosine, sine):
    heads = []
    for i in range(4):
        head = part[:, i * HD : (i + 1) * HD]
        heads.append(head if y == 3 and i >= 2 else turn(head, cosine, sine))
    return jnp.concatenate(heads, axis=1)


def load_parts(layer, w_ref, buf, sem, column, width):
    copies = [
        pltpu.make_async_copy(w_ref.at[:, y, layer, :, pl.ds(column, width)], buf.at[y], sem.at[y])
        for y in range(4)
    ]
    for copy in copies:
        copy.start()
    return copies


def with_parts(ins, weights, width):
    specs = [whole() for _ in ins] + [pl.BlockSpec(memory_space=pltpu.HBM)]
    scratch = [pltpu.VMEM((4, 32, 48, width), BF), pltpu.SemaphoreType.DMA((4,))]
    return list(ins) + [weights], specs, scratch


def cut(refs, count):
    return refs[:count], refs[count], refs[count + 1 : -2], refs[-2], refs[-1]


def project_body(layer, count, *refs):
    lead, w, outs, buf, sem = cut(refs, count)
    copies = load_parts(layer, w, buf, sem, 0, YQ)
    base, gain, cosine, sine = lead[:4]
    h = base[...].astype(F32)
    if count > 4:
        came, high, low = lead[4:]
        rows = came[...]
        h = h + (dot(high[...], rows, NN) + dot(low[...], rows, NN))
        outs[3][...] = h
    attn_in, scale, out = outs[:3]
    factor = lax.rsqrt(jnp.mean(h * h, axis=1, keepdims=True) + norm_epsilon)
    scale[...] = factor
    fed = (h * factor * gain[...]).astype(BF)
    attn_in[...] = fed
    for y in range(4):
        copies[y].wait()
        part = dot(fed, buf[y].reshape(D, -1), NN)
        out[:, y * YQ : (y + 1) * YQ] = rope_heads(part, y, cosine[...], sine[...]).astype(BF)


def project(layer, base, gain, cosine, sine, weights, extra=()):
    lead = [base, gain, cosine, sine, *extra]
    ins, specs, scratch = with_parts(lead, weights, YQ)
    outs = [((TOK, D), BF), ((TOK, 1), F32), ((TOK, QKV), BF)]
    if extra:
        outs = outs + [((TOK, D), F32)]
    return call(
        functools.partial(project_body, layer, len(lead)),
        outs,
        ins,
        specs,
        scratch,
        2 * TOK * D * QKV,
        2 * D * QKV + 8 * TOK * D,
        "project",
    )


def keep_keys(kv_refs, buf):
    for k, ref in enumerate(kv_refs):
        for h in range(2):
            buf[(2 * k + h) * TOK : (2 * k + h + 1) * TOK, :] = ref[h]


def stack_heads(ref, j):
    return jnp.concatenate(
        [ref[:, (j * GROUP + i) * HD : (j * GROUP + i + 1) * HD] for i in range(GROUP)], axis=0
    )


def unstack(total):
    return jnp.concatenate(
        [total[:, i * TOK : (i + 1) * TOK].T for i in range(GROUP)], axis=1
    )


def attend_body(qkv, kv0, kv1, kv2, kv3, key_pos, query_pos, mixed, norm, buf, keep):
    keep_keys((kv0, kv1, kv2, kv3), buf)
    places = jnp.concatenate([query_pos[...]] * GROUP, axis=1)
    for j in range(HK):
        queries = stack_heads(qkv, j)

        def score(b, top):
            at = pl.ds(pl.multiple_of(b * TOK, TOK), TOK)
            keys = buf[at, j * HD : (j + 1) * HD]
            values = dot(keys, queries, NT) * score_scale
            values = jnp.where(key_pos[at, :] <= places, values, -1e30)
            keep[at, :] = values
            return jnp.maximum(top, jnp.max(values, axis=0, keepdims=True))

        top = lax.fori_loop(0, KEYS // TOK, score, jnp.full((1, GT), -1e30, F32))

        def mix(b, carry):
            total, share = carry
            at = pl.ds(pl.multiple_of(b * TOK, TOK), TOK)
            e = jnp.exp(keep[at, :] - top)
            values = buf[at, KW + j * HD : KW + (j + 1) * HD]
            share = share + jnp.sum(e, axis=0, keepdims=True)
            return total + dot(values, e.astype(BF), TN), share

        total, share = lax.fori_loop(
            0, KEYS // TOK, mix, (jnp.zeros((HD, GT), F32), jnp.zeros((1, GT), F32))
        )
        norm[j : j + 1, :] = top + jnp.log(share)
        mixed[:, j * GT : (j + 1) * GT] = unstack(total / share).astype(BF)


def attend(qkv, kv, key_pos, query_pos):
    ins = [qkv, *kv, key_pos, query_pos]
    return call(
        attend_body,
        [((TOK, QW), BF), ((HK, GT), F32)],
        ins,
        [whole() for _ in ins],
        [pltpu.VMEM((KEYS, 2 * KW), BF), pltpu.VMEM((KEYS, GT), F32)],
        4 * TOK * KEYS * QW,
        2 * KEYS * 2 * KW,
        "attend",
    )


def attend_back_body(
    qkv, kv0, kv1, kv2, kv3, key_pos, query_pos, norm, d_mixed, d_queries, d_pairs, buf, kept, given
):
    keep_keys((kv0, kv1, kv2, kv3), buf)
    places = jnp.concatenate([query_pos[...]] * GROUP, axis=1)
    for j in range(HK):
        queries = stack_heads(qkv, j)
        upstream = stack_heads(d_mixed, j)
        level = norm[j : j + 1, :]

        def probs(b, delta):
            at = pl.ds(pl.multiple_of(b * TOK, TOK), TOK)
            keys = buf[at, j * HD : (j + 1) * HD]
            values = buf[at, KW + j * HD : KW + (j + 1) * HD]
            scores = dot(keys, queries, NT) * score_scale
            p = jnp.where(key_pos[at, :] <= places, jnp.exp(scores - level), 0.0)
            dp = dot(values, upstream, NT)
            kept[at, :] = p
            given[at, :] = dp
            d_pairs[at, KW + j * HD : KW + (j + 1) * HD] = dot(p.astype(BF), upstream, NN).astype(BF)
            return delta + jnp.sum(p * dp, axis=0, keepdims=True)

        delta = lax.fori_loop(0, KEYS // TOK, probs, jnp.zeros((1, GT), F32))

        def back(b, total):
            at = pl.ds(pl.multiple_of(b * TOK, TOK), TOK)
            keys = buf[at, j * HD : (j + 1) * HD]
            ds = (kept[at, :] * (given[at, :] - delta)).astype(BF)
            d_pairs[at, j * HD : (j + 1) * HD] = (dot(ds, queries, NN) * score_scale).astype(BF)
            return total + dot(keys, ds, TN)

        total = lax.fori_loop(0, KEYS // TOK, back, jnp.zeros((HD, GT), F32))
        d_queries[:, j * GT : (j + 1) * GT] = unstack(total * score_scale)


def attend_back(qkv, kv, key_pos, query_pos, norm, d_mixed):
    ins = [qkv, *kv, key_pos, query_pos, norm, d_mixed]
    return call(
        attend_back_body,
        [((TOK, QW), F32), ((KEYS, 2 * KW), BF)],
        ins,
        [whole() for _ in ins],
        [pltpu.VMEM((KEYS, 2 * KW), BF), pltpu.VMEM((KEYS, GT), F32), pltpu.VMEM((KEYS, GT), F32)],
        10 * TOK * KEYS * QW,
        4 * KEYS * 2 * KW,
        "attend_back",
    )


def branch_body(layer, *refs):
    (base, mixed, gain, pick), w, (hidden, scale, sent), buf, sem = cut(refs, 4)
    copies = load_parts(layer, w, buf, sem, YQ, YO)
    total = base[...].astype(F32)
    for y in range(4):
        copies[y].wait()
        total = total + dot(mixed[:, y * YO : (y + 1) * YO], buf[y].reshape(D, -1), NT)
    hidden[...] = total
    factor = lax.rsqrt(jnp.mean(total * total, axis=1, keepdims=True) + norm_epsilon)
    scale[...] = factor
    fed = (total * factor * gain[...]).astype(BF)
    sent[...] = dot(pick[...], fed, NN).astype(BF)


def branch(layer, base, mixed, gain, pick, weights):
    ins, specs, scratch = with_parts([base, mixed, gain, pick], weights, YO)
    return call(
        functools.partial(branch_body, layer),
        [((TOK, D), F32), ((TOK, 1), F32), ((ROWS, D), BF)],
        ins,
        specs,
        scratch,
        2 * TOK * D * QW + 2 * TOK * D * ROWS,
        2 * D * QW + 2 * ROWS * D,
        "branch",
    )


BLOCK = 320


def load_expert(w_refs, places, buf, sem):
    copies = []
    for ref in w_refs:
        lead = ref.shape[:-2]
        for at in itertools.product(*[range(n) for n in lead]):
            row = pl.multiple_of(places[len(copies)] * 96, 96)
            copies.append(
                pltpu.make_async_copy(
                    ref.at[at] if at else ref, buf.at[pl.ds(row, 96), :], sem.at[len(copies)]
                )
            )
    for copy in copies:
        copy.start()
    for copy in copies:
        copy.wait()


def gelu_parts(x):
    cdf = 0.5 * (1.0 + lax.erf(x * (0.5**0.5)))
    density = jnp.exp(-0.5 * x * x) * 0.3989422804014327
    return x * cdf, cdf + x * density


def ffn_body(n, places, received, *refs):
    w_refs, (returned, hidden, act, slope, buf, sem) = refs[:n], refs[n:]

    @pl.when(pl.program_id(0) == 0)
    def _():
        load_expert(w_refs, places, buf, sem)

    both = dot(received[...], buf[:, : 2 * FF], NN)
    up = both[:, FF:]
    gelu, gelu_slope = gelu_parts(both[:, :FF])
    low = (gelu * up).astype(BF)
    hidden[...] = low
    act[...] = gelu
    slope[...] = gelu_slope * up
    returned[...] = dot(low, buf[:, 2 * FF :], NT).astype(BF)


def row_block(width):
    return pl.BlockSpec((BLOCK, width), lambda i: (i, 0))


def ffn(received, w_list, places):
    return call(
        functools.partial(ffn_body, len(w_list)),
        [((ROWS, D), BF), ((ROWS, FF), BF), ((ROWS, FF), F32), ((ROWS, FF), F32)],
        [places, received, *w_list],
        [scalars(), row_block(D)] + [anywhere() for _ in w_list],
        [pltpu.VMEM((D, 3 * FF), BF), pltpu.SemaphoreType.DMA((16,))],
        2 * ROWS * D * 3 * FF,
        2 * D * 3 * FF + 16 * ROWS * FF,
        "ffn",
        out_specs=[row_block(D), row_block(FF), row_block(FF), row_block(FF)],
        grid=(ROWS // BLOCK,),
    )


def ffn_back_body(n, places, owner, act, slope, *refs):
    w_refs, (d_rows, d_both, buf, sem) = refs[:n], refs[n:]

    @pl.when(pl.program_id(0) == 0)
    def _():
        load_expert(w_refs, places, buf, sem)

    d_hidden = dot(owner[...], buf[:, 2 * FF :], NN)
    both = jnp.concatenate([d_hidden * slope[...], d_hidden * act[...]], axis=1).astype(BF)
    d_both[...] = both
    d_rows[...] = dot(both, buf[:, : 2 * FF], NT).astype(BF)


def ffn_back(owner, act, slope, w_list, places):
    return call(
        functools.partial(ffn_back_body, len(w_list)),
        [((ROWS, D), BF), ((ROWS, 2 * FF), BF)],
        [places, owner, act, slope, *w_list],
        [scalars(), row_block(D), row_block(FF), row_block(FF)] + [anywhere() for _ in w_list],
        [pltpu.VMEM((D, 3 * FF), BF), pltpu.SemaphoreType.DMA((16,))],
        2 * ROWS * D * 3 * FF,
        2 * D * 3 * FF + 16 * ROWS * FF,
        "ffn_back",
        out_specs=[row_block(D), row_block(2 * FF)],
        grid=(ROWS // BLOCK,),
    )


def ffn_grad_body(received, d_both, owner, hidden, out):
    out[:, 0, :, : 2 * FF] = dot(received[...], d_both[...], TN).astype(BF).reshape(8, 96, 2 * FF)
    out[:, 0, :, 2 * FF :] = dot(owner[...], hidden[...], TN).astype(BF).reshape(8, 96, FF)


def ffn_grad(received, d_both, owner, hidden):
    half = pl.BlockSpec((ROWS, D // 2), lambda i: (0, i))
    fixed = lambda width: pl.BlockSpec((ROWS, width), lambda i: (0, 0))
    return call(
        ffn_grad_body,
        [((8, 2, 96, 3 * FF), BF)],
        [received, d_both, owner, hidden],
        [half, fixed(2 * FF), half, fixed(FF)],
        [],
        2 * ROWS * D * 3 * FF,
        2 * D * 3 * FF + 8 * ROWS * D,
        "ffn_grad",
        out_specs=[pl.BlockSpec((8, 1, 96, 3 * FF), lambda i: (0, i, 0, 0))],
        grid=(2,),
    )[0]


def norm_back(upstream, rows, factor, gain):
    normed = rows * factor
    scaled = upstream * gain
    return (
        factor * (scaled - normed * jnp.mean(scaled * normed, axis=1, keepdims=True)),
        jnp.sum(upstream * normed, axis=0, keepdims=True),
    )


def branch_back_body(layer, *refs):
    lead, w, outs, buf, sem = cut(refs, 6)
    source, pick_t, base, scale, gain, d_out = lead
    d_base, low, d_mixed, d_gain = outs
    copies = load_parts(layer, w, buf, sem, YQ, YO)
    d_fed = dot(pick_t[...], source[...], NN)
    term, d_gain[...] = norm_back(d_fed, base[...], scale[...], gain[...])
    total = d_out[...].astype(F32) + term
    d_base[...] = total
    rounded = total.astype(BF)
    low[...] = rounded
    for y in range(4):
        copies[y].wait()
        d_mixed[:, y * YO : (y + 1) * YO] = dot(rounded, buf[y].reshape(D, -1), NN).astype(BF)


def branch_back(layer, source, pick_t, base, scale, gain, d_out, weights):
    ins, specs, scratch = with_parts([source, pick_t, base, scale, gain, d_out], weights, YO)
    return call(
        functools.partial(branch_back_body, layer),
        [((TOK, D), F32), ((TOK, D), BF), ((TOK, QW), BF), ((1, D), F32)],
        ins,
        specs,
        scratch,
        2 * TOK * D * QW + 2 * TOK * D * ROWS,
        2 * D * QW + 2 * ROWS * D,
        "branch_back",
    )


def project_back_body(layer, count, *refs):
    lead, w, outs, buf, sem = cut(refs, count)
    dq, dkv, cosine, sine, base, scale, gain, d_out = lead[:8]
    d_base, d_proj, d_gain = outs[:3]
    copies = load_parts(layer, w, buf, sem, 0, YQ)
    total = jnp.zeros((TOK, D), F32)
    for y in range(4):
        part = dq[:, y * YQ : (y + 1) * YQ] if y < 3 else dkv[...]
        rounded = rope_heads(part, y, cosine[...], -sine[...]).astype(BF)
        d_proj[:, y * YQ : (y + 1) * YQ] = rounded
        copies[y].wait()
        total = total + dot(rounded, buf[y].reshape(D, -1), NT)
    term, d_gain[...] = norm_back(total, base[...].astype(F32), scale[...], gain[...])
    d_hidden = d_out[...] + term
    d_base[...] = d_hidden
    if count > 8:
        pick, gate = lead[8:]
        high, low = split(d_hidden)
        rows = dot(pick[...], high, NN) + dot(pick[...], low, NN)
        outs[3][...] = (rows * gate[...]).astype(BF)


def project_back(layer, dq, dkv, cosine, sine, base, scale, gain, d_out, weights, extra=()):
    lead = [dq, dkv, cosine, sine, base, scale, gain, d_out, *extra]
    ins, specs, scratch = with_parts(lead, weights, YQ)
    outs = [((TOK, D), F32), ((TOK, QKV), BF), ((1, D), F32)]
    if extra:
        outs = outs + [((ROWS, D), BF)]
    return call(
        functools.partial(project_back_body, layer, len(lead)),
        outs,
        ins,
        specs,
        scratch,
        2 * TOK * D * QKV,
        2 * D * QKV + 8 * TOK * D,
        "project_back",
    )


def wide_grad_body(count, at, *refs):
    own, give = refs[-2:]

    def fill(ref):
        column = 0
        for left, right in zip(refs[:count], refs[count : 2 * count]):
            width = right.shape[1]
            ref[0, :, column : column + width] = dot(left[...], right[...], TN).astype(BF)
            column += width

    pl.when(pl.program_id(0) == 0)(lambda: fill(give))
    pl.when(pl.program_id(0) == 1)(lambda: fill(own))


def wide_grad(at, lefts, rights):
    half = pl.BlockSpec((TOK, D // 2), lambda i, k, at: (0, lax.rem(i + 1 + at[1], 2)))
    column = lambda width: pl.BlockSpec((TOK, width), lambda i, k, at: (0, lax.rem(k + at[0], 4)))
    widths = [right.shape[1] // 4 for right in rights]
    total = sum(widths)
    return pl.pallas_call(
        functools.partial(wide_grad_body, len(lefts)),
        out_shape=[jax.ShapeDtypeStruct((4, D // 2, total), BF)] * 2,
        grid_spec=pltpu.PrefetchScalarGridSpec(
            num_scalar_prefetch=1,
            grid=(2, 4),
            in_specs=[half for _ in lefts] + [column(width) for width in widths],
            out_specs=[
                pl.BlockSpec((1, D // 2, total), lambda i, k, at: (k * i, 0, 0)),
                pl.BlockSpec((1, D // 2, total), lambda i, k, at: (k * (1 - i) + 3 * i, 0, 0)),
            ],
        ),
        compiler_params=pltpu.CompilerParams(vmem_limit_bytes=40 * MIB),
        cost_estimate=pl.CostEstimate(
            flops=8 * TOK * D * total, bytes_accessed=8 * D * total, transcendentals=0
        ),
        name="wide_grad",
    )(at, *lefts, *rights)


def spread_matrices():
    row = jnp.arange(384, dtype=jnp.int32)[:, None]
    column = jnp.arange(768, dtype=jnp.int32)[None, :]
    place = (column // 24) * 12 + column % 12
    late = (column % 24) // 12
    return jnp.stack([((row == place) & (late == h)).astype(BF) for h in range(2)])


def owner_grad_body(at, left, right, spread, own, give):
    width = right.shape[1] // 2
    rows = left[...]
    both = jnp.concatenate([dot(rows, spread[h], NN).astype(BF) for h in range(2)], axis=0)
    sides = jnp.concatenate([right[:, :width], right[:, width:]], axis=0)
    total = dot(both, sides, TN).astype(BF).reshape(32, 24, width)

    def fill(ref):
        ref[...] = total

    pl.when(pl.program_id(0) == 0)(lambda: fill(give))
    pl.when(pl.program_id(0) == 1)(lambda: fill(own))


def owner_grad(at, left, right, spread):
    width = right.shape[1] // 2
    return pl.pallas_call(
        owner_grad_body,
        out_shape=[jax.ShapeDtypeStruct((64, 24, width), BF)] * 2,
        grid_spec=pltpu.PrefetchScalarGridSpec(
            num_scalar_prefetch=1,
            grid=(2, 2),
            in_specs=[
                pl.BlockSpec((TOK, 384), lambda i, s, at: (0, lax.rem(i + 1 + at[1], 2) * 2 + s)),
                pl.BlockSpec((TOK, 2 * width), lambda i, s, at: (0, 0)),
                pl.BlockSpec((2, 384, 768), lambda i, s, at: (0, 0, 0)),
            ],
            out_specs=[
                pl.BlockSpec((32, 24, width), lambda i, s, at: (s * i, 0, 0)),
                pl.BlockSpec((32, 24, width), lambda i, s, at: (s * (1 - i) + i, 0, 0)),
            ],
        ),
        compiler_params=pltpu.CompilerParams(vmem_limit_bytes=40 * MIB),
        cost_estimate=pl.CostEstimate(
            flops=4 * TOK * D * 2 * width, bytes_accessed=4 * D * width, transcendentals=0
        ),
        name="owner_grad",
    )(at, left, right, spread)


beta_first = 0.9
beta_second = 0.95
adam_epsilon = 1e-08
gain_rate = 3.0
matrix_decay = 0.1
rope_base = 10000.0
ALL = ("dp", "context", "experts")
OWNERS = ("dp", "experts")
LINE = ("context", "experts")
Y_GROUPS = [[0, 1, 2, 3], [4, 5, 6, 7]]


def send_z(value, hop):
    pairs = [(z * 2 + h, ((z + hop) % 4) * 2 + h) for z in range(4) for h in range(2)]
    return lax.ppermute(value, "context", pairs)


def swap_xh(value):
    pairs = [(z * 2 + h, z * 2 + 1 - h) for z in range(4) for h in range(2)]
    return lax.ppermute(value, "context", pairs)


def send_y(value, hop):
    pairs = [(l * 4 + y, l * 4 + (y + hop) % 4) for l in range(2) for y in range(4)]
    return lax.ppermute(value, "experts", pairs)


def swap_xl(value):
    pairs = [(l * 4 + y, (1 - l) * 4 + y) for l in range(2) for y in range(4)]
    return lax.ppermute(value, "experts", pairs)


def swap_core(value):
    return lax.ppermute(value, "dp", [(0, 1), (1, 0)])


def place():
    context = lax.axis_index("context")
    experts = lax.axis_index("experts")
    return dict(d=lax.axis_index("dp"), z=context // 2, xh=context % 2, xl=experts // 4, y=experts % 4)


def ordered(flag, own, other):
    return jnp.where(flag == 0, jnp.stack([own, other]), jnp.stack([other, own]))


def keep_and_give(pair, flag):
    return (
        lax.dynamic_index_in_dim(pair, flag, 0, False),
        lax.dynamic_index_in_dim(pair, 1 - flag, 0, False),
    )


def rope_tables(positions):
    frequency = rope_base ** (jnp.arange(HD // 2, dtype=F32) * (-2.0 / HD))
    angles = positions.astype(F32)[:, None] * frequency[None, :]
    cosine, sine = jnp.cos(angles), jnp.sin(angles)
    return jnp.concatenate([cosine, cosine], axis=1), jnp.concatenate([-sine, sine], axis=1)


def adam_update(weight, first_moment, second_moment, gradient, step_rate, decay_term):
    first_new = beta_first * first_moment + (1.0 - beta_first) * gradient
    second_new = beta_second * second_moment + (1.0 - beta_second) * gradient * gradient
    first_hat = first_new / (1.0 - beta_first**STEP)
    second_hat = second_new / (1.0 - beta_second**STEP)
    weight_new = weight - step_rate * (
        first_hat / (jnp.sqrt(second_hat) + adam_epsilon) + decay_term * weight
    )
    return (weight_new, first_new, second_new)


def routing(ids, gates):
    flat = ids.reshape(-1)
    one_hot = (flat[:, None] == jnp.arange(EXPERTS, dtype=jnp.int32)).astype(jnp.int32)
    earlier = jnp.cumsum(one_hot, axis=0) - one_hot
    rank = jnp.sum(earlier * one_hot, axis=-1)
    owner = (flat % 2) * (EXPERTS // 2) + flat // 2
    slots = (owner * CAP + rank).reshape(ids.shape)
    hit = slots[:, :, None] == jnp.arange(ROWS, dtype=jnp.int32)
    pick = jnp.any(hit, axis=1).astype(BF)
    weight = jnp.sum(jnp.where(hit, gates[:, :, None], 0.0), axis=1)
    slot_gate = jnp.sum(weight, axis=0)[:, None]
    weight_high, weight_low = split(weight)
    return pick, pick.T, weight_high, weight_low, slot_gate


def exchange(rows):
    return lax.all_to_all(
        rows.reshape(EXPERTS, CAP, D), OWNERS, split_axis=0, concat_axis=0, tiled=True
    ).reshape(ROWS, D)


def gather_keys(rows):
    pair = ordered(place()["xh"], rows, swap_xh(rows))
    return [pair] + [send_z(pair, k) for k in (1, 2, 3)]


def return_keys(grads):
    total = grads[0].astype(F32)
    for k in (1, 2, 3):
        total = total + send_z(grads[k], -k).astype(F32)
    own, other = keep_and_give(total, place()["xh"])
    return own + swap_xh(other.astype(BF)).astype(F32)


def column_blocks(qkv_weight, out_weight):
    return jnp.concatenate(
        [
            qkv_weight.astype(BF).reshape(LAYERS, -1, 4, YQ),
            out_weight.astype(BF).transpose(0, 2, 1).reshape(LAYERS, -1, 4, YO),
        ],
        axis=-1,
    ).transpose(2, 0, 1, 3)


def core_pair(in_weight, down_weight):
    both = jnp.concatenate(
        [in_weight.astype(BF), down_weight.astype(BF).transpose(0, 2, 1)], axis=-1
    )
    own, give = keep_and_give(both, lax.axis_index("dp"))
    return own, swap_core(give)


def add_cores(grads):
    own, give = grads
    return (own.astype(F32) + swap_core(give).astype(F32)).astype(BF)


def wide_send(half):
    return [half[0]] + [send_y(half[k], k) for k in (1, 2, 3)]


def line_z(rows):
    z = place()["z"]
    cut = rows.reshape(4, 192, -1)
    total = lax.dynamic_index_in_dim(cut, z, 0, False).astype(F32)
    for k in (1, 2, 3):
        piece = lax.dynamic_index_in_dim(cut, (z + k) % 4, 0, False)
        total = total + send_z(piece, k).astype(F32)
    return total.astype(rows.dtype)


def line_swaps(rows):
    at = place()
    for flag, swap, count in ((at["xh"], swap_xh, 96), (at["xl"], swap_xl, 48)):
        kept, other = keep_and_give(rows.reshape(2, count, -1), flag)
        rows = (kept.astype(F32) + swap(other).astype(F32)).astype(rows.dtype)
    return rows


def spread_line(rows):
    y = place()["y"]
    pieces = rows.reshape(4, 12, -1)
    got = [lax.dynamic_index_in_dim(pieces, y, 0, False)] + [
        send_y(lax.dynamic_index_in_dim(pieces, (y + k) % 4, 0, False), k) for k in (1, 2, 3)
    ]
    order = (y - jnp.arange(4, dtype=jnp.int32)) % 4
    return jnp.take(jnp.stack(got), order, axis=0).astype(F32).transpose(1, 0, 2)


def owner_sum(parts):
    total = jnp.sum(parts.astype(F32), axis=0)
    return jnp.concatenate([total[:12], total[12:]], axis=1)


def scatter_experts(grads):
    pair = lax.psum_scatter(grads, "context", scatter_dimension=0)
    core = lax.axis_index("dp")
    own, give = keep_and_give(pair, core)
    return ordered(core, own, swap_core(give)).astype(F32)


def local(
    tokens,
    cotangent,
    expert_ids,
    gate_values,
    block_order,
    qkv_weight,
    qkv_first,
    qkv_second,
    out_weight,
    out_first,
    out_second,
    in_weight,
    in_first,
    in_second,
    down_weight,
    down_first,
    down_second,
    norm_gains,
    gain_first,
    gain_second,
):
    at = place()
    wide_at = jnp.stack([at["y"], at["d"]]).astype(jnp.int32)
    rows = lax.all_to_all(
        column_blocks(qkv_weight, out_weight),
        "experts",
        0,
        0,
        axis_index_groups=Y_GROUPS,
        tiled=True,
    )
    rows = rows.transpose(1, 0, 2, 3).reshape(LAYERS, 48, YQ + YO)
    projections = [
        lax.all_gather(rows[l], ALL, axis=0).reshape(32, 4, 1, 48, YQ + YO) for l in range(LAYERS)
    ]
    gain_rows = norm_gains.astype(BF).astype(F32).reshape(1, 1, 48)
    gains = lax.all_to_all(jnp.broadcast_to(gain_rows, (128, 1, 48)), ALL, 0, 0, tiled=True)
    gains = gains.reshape(128, 4, 12).transpose(1, 0, 2).reshape(4, 1, D)
    own, other = core_pair(in_weight[0], down_weight[0])
    column = [own] + [send_z(own, k) for k in (1, 2, 3)]
    beside = [swap_xh(part) for part in column]
    pair = ordered(at["xh"], other, swap_xh(other))
    pairs = [pair] + [send_z(pair, k) for k in (1, 2, 3)]
    later = ordered(at["d"], *core_pair(in_weight[1], down_weight[1]))
    gathered = lax.all_gather(later, "context", axis=0)
    turns = (at["z"] - jnp.arange(4, dtype=jnp.int32)) % 4
    both = jnp.arange(2, dtype=jnp.int32)
    chunk_places = jnp.concatenate(
        [
            at["d"] * 8 + turns * 2 + at["xh"],
            at["d"] * 8 + turns * 2 + 1 - at["xh"],
            ((1 - at["d"]) * 8 + turns[:, None] * 2 + both[None, :]).reshape(-1),
        ]
    ).astype(jnp.int32)
    gathered_places = (jnp.arange(8, dtype=jnp.int32)[:, None] + 8 * both[None, :]).reshape(-1)
    experts = [(column + beside + pairs, chunk_places), ([gathered], gathered_places)]

    order_row = block_order[0]
    offsets = jnp.arange(TOK, dtype=jnp.int32)
    places = jnp.arange(8, dtype=jnp.int32)
    source = (turns[:, None] * 2 + both[None, :]).reshape(-1)
    key_block = jnp.sum(jnp.where(source[:, None] == places, order_row, 0), axis=1)
    own_block = jnp.sum(jnp.where(places == lax.axis_index("context"), order_row, 0))
    query_pos = own_block * TOK + offsets
    key_pos = (key_block[:, None] * TOK + offsets[None, :]).reshape(-1, 1)
    cosine, sine = rope_tables(query_pos)
    query_pos = query_pos.reshape(1, -1)
    routes = [routing(expert_ids[l, 0], gate_values[l, 0]) for l in range(LAYERS)]
    spread = spread_matrices()
    cotangent_rows = (dot(routes[-1][1], cotangent[0], NN) * routes[-1][4]).astype(BF)
    start, last_owner = lax.optimization_barrier((tokens[0], exchange(cotangent_rows)))
    saved = []
    base, came_back = start, ()
    for l in range(LAYERS):
        pick, pick_t, weight_high, weight_low, slot_gate = routes[l]
        attn_in, scale_one, qkv, *rest = project(
            0, base, gains[2 * l], cosine, sine, projections[l], came_back
        )
        if l:
            base = rest[0]
        kv = gather_keys(qkv[:, QW:])
        mixed, level = attend(qkv, kv, key_pos, query_pos)
        middle, scale_two, sent = branch(
            0, base, mixed, gains[2 * l + 1], pick_t, projections[l]
        )
        received = exchange(sent)
        returned, hidden, act, slope = ffn(received, *experts[l])
        if l == 0:
            came_back = (exchange(returned), weight_high, weight_low)
        saved.append(
            (base, attn_in, scale_one, qkv, kv, mixed, level, middle, scale_two, received, hidden, act, slope)
        )
        base = middle
    d_out = cotangent[0]
    expert_sums = [None] * LAYERS
    gain_grads = [None] * (2 * LAYERS)
    for l in reversed(range(LAYERS)):
        (base, attn_in, scale_one, qkv, kv, mixed, level, middle, scale_two, received, hidden, act, slope) = (
            saved[l]
        )
        if l == LAYERS - 1:
            owner = last_owner
        else:
            owner, wide_half = lax.optimization_barrier((exchange(sent), wide_half))
            wide_parts = wide_send(wide_half)
        d_rows, d_both = ffn_back(owner, act, slope, *experts[l])
        came_grad, expert_grad = lax.optimization_barrier(
            (exchange(d_rows), ffn_grad(received, d_both, owner, hidden))
        )
        if l == LAYERS - 1:
            returned, came_grad = lax.optimization_barrier((returned, came_grad))
            returned = exchange(returned)
        else:
            expert_grad, expert_sums[l + 1] = lax.optimization_barrier(
                (expert_grad, expert_sums[l + 1])
            )
        expert_sums[l] = scatter_experts(expert_grad)
        d_base, d_branch, d_mixed, gain_grads[2 * l + 1] = branch_back(
            0,
            came_grad, routes[l][0], middle, scale_two, gains[2 * l + 1], d_out, projections[l]
        )
        if l == 0:
            out_half = add_cores(owner_grad(wide_at, d_branch, mixed, spread))
            out_parts = lax.all_to_all(out_half, LINE, 0, 0, tiled=True)
        d_queries, d_pairs = attend_back(qkv, kv, key_pos, query_pos, level, d_mixed)
        if l == 0:
            d_pairs, wide_parts[1], wide_parts[3] = lax.optimization_barrier(
                (d_pairs, wide_parts[1], wide_parts[3])
            )
        d_key_value = return_keys(d_pairs.reshape(4, 2, TOK, 2 * KW))
        if l == LAYERS - 1:
            d_key_value, returned = lax.optimization_barrier((d_key_value, returned))
            result = middle + dot(routes[l][2], returned, NN) + dot(routes[l][3], returned, NN)
        else:
            d_key_value, out_parts, wide_parts = lax.optimization_barrier(
                (d_key_value, out_parts, wide_parts)
            )
        extra = (routes[l - 1][1], routes[l - 1][4]) if l else ()
        back = project_back(
            0,
            d_queries,
            d_key_value,
            cosine,
            sine,
            base,
            scale_one,
            gains[2 * l],
            d_base,
            projections[l],
            extra,
        )
        d_out, d_projected, gain_grads[2 * l] = back[:3]
        if l:
            sent = back[3]
            wide_half = add_cores(wide_grad(wide_at, [attn_in, d_branch], [d_projected, mixed]))
        else:
            qkv_half = add_cores(owner_grad(wide_at, attn_in, d_projected, spread))
            wide_line = line_z(sum(part.astype(F32) for part in wide_parts).astype(BF))
            wide_rows = spread_line(line_swaps(wide_line))
    qkv_parts = lax.all_to_all(qkv_half, LINE, 0, 0, tiled=True)
    gain_rows = jnp.concatenate(gain_grads, axis=0).reshape(4, 128, 12)
    gain_rows = gain_rows.transpose(1, 0, 2).reshape(128, 1, 48)
    gain_rows, qkv_parts = lax.optimization_barrier((gain_rows, qkv_parts))
    gain_sum = jnp.sum(lax.all_to_all(gain_rows, ALL, 0, 0, tiled=True), axis=0).reshape(2, 2, 12)
    qkv_sum = jnp.stack([owner_sum(qkv_parts), wide_rows[:, :, :YQ].reshape(12, QKV)], axis=1)
    out_sum = jnp.stack([owner_sum(out_parts), wide_rows[:, :, YQ:].reshape(12, QW)], axis=1)
    in_sum = jnp.stack([s[:, :, : 2 * FF] for s in expert_sums])
    down_sum = jnp.stack([s[:, :, 2 * FF :] for s in expert_sums]).transpose(0, 1, 3, 2)
    wide_rate = 5.0 * D ** (-0.5)
    out_rate = 5.0 * (HQ * HD / 16.0) ** (-0.5)
    down_rate = 5.0 * (FF / 4.0) ** (-0.5)
    qkv_state = [v.transpose(1, 0, 2) for v in (qkv_weight, qkv_first, qkv_second)]
    out_state = [v.transpose(2, 0, 1) for v in (out_weight, out_first, out_second)]
    qkv_update = adam_update(*qkv_state, qkv_sum, wide_rate, matrix_decay)
    out_update = adam_update(*out_state, out_sum, out_rate, matrix_decay)
    updates = (
        tuple(v.transpose(1, 0, 2) for v in qkv_update)
        + tuple(v.transpose(1, 2, 0) for v in out_update)
        + adam_update(in_weight, in_first, in_second, in_sum, wide_rate, matrix_decay)
        + adam_update(down_weight, down_first, down_second, down_sum, down_rate, matrix_decay)
        + adam_update(norm_gains, gain_first, gain_second, gain_sum, gain_rate, 0.0)
    )
    return (result.astype(BF)[None], d_out[None]) + updates


def solution(mesh):
    rows = P(("dp", "experts"), "context", None)
    routes = P(None, ("dp", "experts"), "context", None)
    qkv = P(None, ALL, None)
    out = P(None, None, ALL)
    wide = P(None, "experts", ("dp", "context"), None)
    down = P(None, "experts", None, ("dp", "context"))
    states = (qkv,) * 3 + (out,) * 3 + (wide,) * 3 + (down,) * 3 + (out,) * 3
    return jax.shard_map(
        local,
        mesh=mesh,
        in_specs=(rows, rows, routes, routes, P(("dp", "experts"), None)) + states,
        out_specs=(rows, rows) + states,
        check_vma=False,
    )
```

```python
import functools
import itertools
import jax
import jax.numpy as jnp
from jax import lax
from jax.experimental import pallas as pl
from jax.experimental.pallas import tpu as pltpu
from jax.sharding import PartitionSpec as P

D = 1536
HQ = 12
HK = 2
HD = 128
FF = 768
TOP = 4
LAYERS = 2
STEP = 5
EXPERTS = 16
CAP = 40
ROWS = EXPERTS * CAP
QKV = (HQ + 2 * HK) * HD
QW = HQ * HD
KW = HK * HD
YQ = QKV // 4
YO = QW // 4
TOK = 128
KEYS = 1024
GROUP = HQ // HK
GT = GROUP * TOK
score_scale = HD ** (-0.5)
norm_epsilon = 1e-06
BF = jnp.bfloat16
F32 = jnp.float32
MIB = 1 << 20


def dot(a, b, contract):
    return lax.dot_general(a, b, (contract, ((), ())), preferred_element_type=F32)


NN = ((1,), (0,))
NT = ((1,), (1,))
TN = ((0,), (0,))


def split(value):
    high = value.astype(BF)
    return high, (value - high.astype(F32)).astype(BF)


def whole():
    return pl.BlockSpec(memory_space=pltpu.VMEM)


def scalars():
    return pl.BlockSpec(memory_space=pltpu.SMEM)


def anywhere():
    return pl.BlockSpec(memory_space=pltpu.HBM)


def call(body, outs, ins, specs, scratch, flops, moved, name, mib=40, out_specs=None, grid=None):
    return pl.pallas_call(
        body,
        out_shape=[jax.ShapeDtypeStruct(s, t) for s, t in outs],
        in_specs=specs,
        out_specs=out_specs or [whole() for _ in outs],
        scratch_shapes=scratch,
        grid=grid or (),
        compiler_params=pltpu.CompilerParams(vmem_limit_bytes=mib * MIB),
        cost_estimate=pl.CostEstimate(flops=int(flops), bytes_accessed=int(moved), transcendentals=0),
        name=name,
    )(*ins)


def turn(head, cosine, sine):
    return head * cosine + pltpu.roll(head, HD // 2, 1) * sine


def rope_heads(part, y, cosine, sine):
    heads = []
    for i in range(4):
        head = part[:, i * HD : (i + 1) * HD]
        heads.append(head if y == 3 and i >= 2 else turn(head, cosine, sine))
    return jnp.concatenate(heads, axis=1)


def load_parts(layer, w_ref, buf, sem, column, width):
    copies = [
        pltpu.make_async_copy(w_ref.at[:, y, layer, :, pl.ds(column, width)], buf.at[y], sem.at[y])
        for y in range(4)
    ]
    for copy in copies:
        copy.start()
    return copies


def with_parts(ins, weights, width):
    specs = [whole() for _ in ins] + [pl.BlockSpec(memory_space=pltpu.HBM)]
    scratch = [pltpu.VMEM((4, 32, 48, width), BF), pltpu.SemaphoreType.DMA((4,))]
    return list(ins) + [weights], specs, scratch


def cut(refs, count):
    return refs[:count], refs[count], refs[count + 1 : -2], refs[-2], refs[-1]


def project_body(layer, count, *refs):
    lead, w, outs, buf, sem = cut(refs, count)
    copies = load_parts(layer, w, buf, sem, 0, YQ)
    base, gain, cosine, sine = lead[:4]
    h = base[...].astype(F32)
    if count > 4:
        came, high, low = lead[4:]
        rows = came[...]
        h = h + (dot(high[...], rows, NN) + dot(low[...], rows, NN))
        outs[3][...] = h
    attn_in, scale, out = outs[:3]
    factor = lax.rsqrt(jnp.mean(h * h, axis=1, keepdims=True) + norm_epsilon)
    scale[...] = factor
    fed = (h * factor * gain[...]).astype(BF)
    attn_in[...] = fed
    for y in range(4):
        copies[y].wait()
        part = dot(fed, buf[y].reshape(D, -1), NN)
        out[:, y * YQ : (y + 1) * YQ] = rope_heads(part, y, cosine[...], sine[...]).astype(BF)


def project(layer, base, gain, cosine, sine, weights, extra=()):
    lead = [base, gain, cosine, sine, *extra]
    ins, specs, scratch = with_parts(lead, weights, YQ)
    outs = [((TOK, D), BF), ((TOK, 1), F32), ((TOK, QKV), BF)]
    if extra:
        outs = outs + [((TOK, D), F32)]
    return call(
        functools.partial(project_body, layer, len(lead)),
        outs,
        ins,
        specs,
        scratch,
        2 * TOK * D * QKV,
        2 * D * QKV + 8 * TOK * D,
        "project",
    )


def keep_keys(kv_refs, buf):
    for k, ref in enumerate(kv_refs):
        for h in range(2):
            buf[(2 * k + h) * TOK : (2 * k + h + 1) * TOK, :] = ref[h]


def stack_heads(ref, j):
    return jnp.concatenate(
        [ref[:, (j * GROUP + i) * HD : (j * GROUP + i + 1) * HD] for i in range(GROUP)], axis=0
    )


def unstack(total):
    return jnp.concatenate(
        [total[:, i * TOK : (i + 1) * TOK].T for i in range(GROUP)], axis=1
    )


def attend_body(qkv, kv0, kv1, kv2, kv3, key_pos, query_pos, mixed, norm, buf, keep):
    keep_keys((kv0, kv1, kv2, kv3), buf)
    places = jnp.concatenate([query_pos[...]] * GROUP, axis=1)
    for j in range(HK):
        queries = stack_heads(qkv, j)

        def score(b, top):
            at = pl.ds(pl.multiple_of(b * TOK, TOK), TOK)
            keys = buf[at, j * HD : (j + 1) * HD]
            values = dot(keys, queries, NT) * score_scale
            values = jnp.where(key_pos[at, :] <= places, values, -1e30)
            keep[at, :] = values
            return jnp.maximum(top, jnp.max(values, axis=0, keepdims=True))

        top = lax.fori_loop(0, KEYS // TOK, score, jnp.full((1, GT), -1e30, F32))

        def mix(b, carry):
            total, share = carry
            at = pl.ds(pl.multiple_of(b * TOK, TOK), TOK)
            e = jnp.exp(keep[at, :] - top)
            values = buf[at, KW + j * HD : KW + (j + 1) * HD]
            share = share + jnp.sum(e, axis=0, keepdims=True)
            return total + dot(values, e.astype(BF), TN), share

        total, share = lax.fori_loop(
            0, KEYS // TOK, mix, (jnp.zeros((HD, GT), F32), jnp.zeros((1, GT), F32))
        )
        norm[j : j + 1, :] = top + jnp.log(share)
        mixed[:, j * GT : (j + 1) * GT] = unstack(total / share).astype(BF)


def attend(qkv, kv, key_pos, query_pos):
    ins = [qkv, *kv, key_pos, query_pos]
    return call(
        attend_body,
        [((TOK, QW), BF), ((HK, GT), F32)],
        ins,
        [whole() for _ in ins],
        [pltpu.VMEM((KEYS, 2 * KW), BF), pltpu.VMEM((KEYS, GT), F32)],
        4 * TOK * KEYS * QW,
        2 * KEYS * 2 * KW,
        "attend",
    )


def attend_back_body(
    qkv, kv0, kv1, kv2, kv3, key_pos, query_pos, norm, d_mixed, d_queries, d_pairs, buf, kept, given
):
    keep_keys((kv0, kv1, kv2, kv3), buf)
    places = jnp.concatenate([query_pos[...]] * GROUP, axis=1)
    for j in range(HK):
        queries = stack_heads(qkv, j)
        upstream = stack_heads(d_mixed, j)
        level = norm[j : j + 1, :]

        def probs(b, delta):
            at = pl.ds(pl.multiple_of(b * TOK, TOK), TOK)
            keys = buf[at, j * HD : (j + 1) * HD]
            values = buf[at, KW + j * HD : KW + (j + 1) * HD]
            scores = dot(keys, queries, NT) * score_scale
            p = jnp.where(key_pos[at, :] <= places, jnp.exp(scores - level), 0.0)
            dp = dot(values, upstream, NT)
            kept[at, :] = p
            given[at, :] = dp
            d_pairs[at, KW + j * HD : KW + (j + 1) * HD] = dot(p.astype(BF), upstream, NN).astype(BF)
            return delta + jnp.sum(p * dp, axis=0, keepdims=True)

        delta = lax.fori_loop(0, KEYS // TOK, probs, jnp.zeros((1, GT), F32))

        def back(b, total):
            at = pl.ds(pl.multiple_of(b * TOK, TOK), TOK)
            keys = buf[at, j * HD : (j + 1) * HD]
            ds = (kept[at, :] * (given[at, :] - delta)).astype(BF)
            d_pairs[at, j * HD : (j + 1) * HD] = (dot(ds, queries, NN) * score_scale).astype(BF)
            return total + dot(keys, ds, TN)

        total = lax.fori_loop(0, KEYS // TOK, back, jnp.zeros((HD, GT), F32))
        d_queries[:, j * GT : (j + 1) * GT] = unstack(total * score_scale)


def attend_back(qkv, kv, key_pos, query_pos, norm, d_mixed):
    ins = [qkv, *kv, key_pos, query_pos, norm, d_mixed]
    return call(
        attend_back_body,
        [((TOK, QW), F32), ((KEYS, 2 * KW), BF)],
        ins,
        [whole() for _ in ins],
        [pltpu.VMEM((KEYS, 2 * KW), BF), pltpu.VMEM((KEYS, GT), F32), pltpu.VMEM((KEYS, GT), F32)],
        10 * TOK * KEYS * QW,
        4 * KEYS * 2 * KW,
        "attend_back",
    )


def branch_body(layer, *refs):
    (base, mixed, gain, pick), w, (hidden, scale, sent), buf, sem = cut(refs, 4)
    copies = load_parts(layer, w, buf, sem, YQ, YO)
    total = base[...].astype(F32)
    for y in range(4):
        copies[y].wait()
        total = total + dot(mixed[:, y * YO : (y + 1) * YO], buf[y].reshape(D, -1), NT)
    hidden[...] = total
    factor = lax.rsqrt(jnp.mean(total * total, axis=1, keepdims=True) + norm_epsilon)
    scale[...] = factor
    fed = (total * factor * gain[...]).astype(BF)
    sent[...] = dot(pick[...], fed, NN).astype(BF)


def branch(layer, base, mixed, gain, pick, weights):
    ins, specs, scratch = with_parts([base, mixed, gain, pick], weights, YO)
    return call(
        functools.partial(branch_body, layer),
        [((TOK, D), F32), ((TOK, 1), F32), ((ROWS, D), BF)],
        ins,
        specs,
        scratch,
        2 * TOK * D * QW + 2 * TOK * D * ROWS,
        2 * D * QW + 2 * ROWS * D,
        "branch",
    )


BLOCK = 320


def load_expert(w_refs, places, buf, sem):
    copies = []
    for ref in w_refs:
        lead = ref.shape[:-2]
        for at in itertools.product(*[range(n) for n in lead]):
            row = pl.multiple_of(places[len(copies)] * 96, 96)
            copies.append(
                pltpu.make_async_copy(
                    ref.at[at] if at else ref, buf.at[pl.ds(row, 96), :], sem.at[len(copies)]
                )
            )
    for copy in copies:
        copy.start()
    for copy in copies:
        copy.wait()


def gelu_parts(x):
    cdf = 0.5 * (1.0 + lax.erf(x * (0.5**0.5)))
    density = jnp.exp(-0.5 * x * x) * 0.3989422804014327
    return x * cdf, cdf + x * density


def ffn_body(n, places, received, *refs):
    w_refs, (returned, hidden, act, slope, buf, sem) = refs[:n], refs[n:]

    @pl.when(pl.program_id(0) == 0)
    def _():
        load_expert(w_refs, places, buf, sem)

    both = dot(received[...], buf[:, : 2 * FF], NN)
    up = both[:, FF:]
    gelu, gelu_slope = gelu_parts(both[:, :FF])
    low = (gelu * up).astype(BF)
    hidden[...] = low
    act[...] = gelu
    slope[...] = gelu_slope * up
    returned[...] = dot(low, buf[:, 2 * FF :], NT).astype(BF)


def row_block(width):
    return pl.BlockSpec((BLOCK, width), lambda i: (i, 0))


def ffn(received, w_list, places):
    return call(
        functools.partial(ffn_body, len(w_list)),
        [((ROWS, D), BF), ((ROWS, FF), BF), ((ROWS, FF), F32), ((ROWS, FF), F32)],
        [places, received, *w_list],
        [scalars(), row_block(D)] + [anywhere() for _ in w_list],
        [pltpu.VMEM((D, 3 * FF), BF), pltpu.SemaphoreType.DMA((16,))],
        2 * ROWS * D * 3 * FF,
        2 * D * 3 * FF + 16 * ROWS * FF,
        "ffn",
        out_specs=[row_block(D), row_block(FF), row_block(FF), row_block(FF)],
        grid=(ROWS // BLOCK,),
    )


def ffn_back_body(n, places, owner, act, slope, *refs):
    w_refs, (d_rows, d_both, buf, sem) = refs[:n], refs[n:]

    @pl.when(pl.program_id(0) == 0)
    def _():
        load_expert(w_refs, places, buf, sem)

    d_hidden = dot(owner[...], buf[:, 2 * FF :], NN)
    both = jnp.concatenate([d_hidden * slope[...], d_hidden * act[...]], axis=1).astype(BF)
    d_both[...] = both
    d_rows[...] = dot(both, buf[:, : 2 * FF], NT).astype(BF)


def ffn_back(owner, act, slope, w_list, places):
    return call(
        functools.partial(ffn_back_body, len(w_list)),
        [((ROWS, D), BF), ((ROWS, 2 * FF), BF)],
        [places, owner, act, slope, *w_list],
        [scalars(), row_block(D), row_block(FF), row_block(FF)] + [anywhere() for _ in w_list],
        [pltpu.VMEM((D, 3 * FF), BF), pltpu.SemaphoreType.DMA((16,))],
        2 * ROWS * D * 3 * FF,
        2 * D * 3 * FF + 16 * ROWS * FF,
        "ffn_back",
        out_specs=[row_block(D), row_block(2 * FF)],
        grid=(ROWS // BLOCK,),
    )


def ffn_grad_body(received, d_both, owner, hidden, out):
    out[:, 0, :, : 2 * FF] = dot(received[...], d_both[...], TN).astype(BF).reshape(8, 96, 2 * FF)
    out[:, 0, :, 2 * FF :] = dot(owner[...], hidden[...], TN).astype(BF).reshape(8, 96, FF)


def ffn_grad(received, d_both, owner, hidden):
    half = pl.BlockSpec((ROWS, D // 2), lambda i: (0, i))
    fixed = lambda width: pl.BlockSpec((ROWS, width), lambda i: (0, 0))
    return call(
        ffn_grad_body,
        [((8, 2, 96, 3 * FF), BF)],
        [received, d_both, owner, hidden],
        [half, fixed(2 * FF), half, fixed(FF)],
        [],
        2 * ROWS * D * 3 * FF,
        2 * D * 3 * FF + 8 * ROWS * D,
        "ffn_grad",
        out_specs=[pl.BlockSpec((8, 1, 96, 3 * FF), lambda i: (0, i, 0, 0))],
        grid=(2,),
    )[0]


def norm_back(upstream, rows, factor, gain):
    normed = rows * factor
    scaled = upstream * gain
    return (
        factor * (scaled - normed * jnp.mean(scaled * normed, axis=1, keepdims=True)),
        jnp.sum(upstream * normed, axis=0, keepdims=True),
    )


def branch_back_body(layer, *refs):
    lead, w, outs, buf, sem = cut(refs, 6)
    source, pick_t, base, scale, gain, d_out = lead
    d_base, low, d_mixed, d_gain = outs
    copies = load_parts(layer, w, buf, sem, YQ, YO)
    d_fed = dot(pick_t[...], source[...], NN)
    term, d_gain[...] = norm_back(d_fed, base[...], scale[...], gain[...])
    total = d_out[...].astype(F32) + term
    d_base[...] = total
    rounded = total.astype(BF)
    low[...] = rounded
    for y in range(4):
        copies[y].wait()
        d_mixed[:, y * YO : (y + 1) * YO] = dot(rounded, buf[y].reshape(D, -1), NN).astype(BF)


def branch_back(layer, source, pick_t, base, scale, gain, d_out, weights):
    ins, specs, scratch = with_parts([source, pick_t, base, scale, gain, d_out], weights, YO)
    return call(
        functools.partial(branch_back_body, layer),
        [((TOK, D), F32), ((TOK, D), BF), ((TOK, QW), BF), ((1, D), F32)],
        ins,
        specs,
        scratch,
        2 * TOK * D * QW + 2 * TOK * D * ROWS,
        2 * D * QW + 2 * ROWS * D,
        "branch_back",
    )


def project_back_body(layer, count, *refs):
    lead, w, outs, buf, sem = cut(refs, count)
    dq, dkv, cosine, sine, base, scale, gain, d_out = lead[:8]
    d_base, d_proj, d_gain = outs[:3]
    copies = load_parts(layer, w, buf, sem, 0, YQ)
    total = jnp.zeros((TOK, D), F32)
    for y in range(4):
        part = dq[:, y * YQ : (y + 1) * YQ] if y < 3 else dkv[...]
        rounded = rope_heads(part, y, cosine[...], -sine[...]).astype(BF)
        d_proj[:, y * YQ : (y + 1) * YQ] = rounded
        copies[y].wait()
        total = total + dot(rounded, buf[y].reshape(D, -1), NT)
    term, d_gain[...] = norm_back(total, base[...].astype(F32), scale[...], gain[...])
    d_hidden = d_out[...] + term
    d_base[...] = d_hidden
    if count > 8:
        pick, gate = lead[8:]
        high, low = split(d_hidden)
        rows = dot(pick[...], high, NN) + dot(pick[...], low, NN)
        outs[3][...] = (rows * gate[...]).astype(BF)


def project_back(layer, dq, dkv, cosine, sine, base, scale, gain, d_out, weights, extra=()):
    lead = [dq, dkv, cosine, sine, base, scale, gain, d_out, *extra]
    ins, specs, scratch = with_parts(lead, weights, YQ)
    outs = [((TOK, D), F32), ((TOK, QKV), BF), ((1, D), F32)]
    if extra:
        outs = outs + [((ROWS, D), BF)]
    return call(
        functools.partial(project_back_body, layer, len(lead)),
        outs,
        ins,
        specs,
        scratch,
        2 * TOK * D * QKV,
        2 * D * QKV + 8 * TOK * D,
        "project_back",
    )


def wide_grad_body(count, at, *refs):
    own, give = refs[-2:]

    def fill(ref):
        column = 0
        for left, right in zip(refs[:count], refs[count : 2 * count]):
            width = right.shape[1]
            ref[0, :, column : column + width] = dot(left[...], right[...], TN).astype(BF)
            column += width

    pl.when(pl.program_id(0) == 0)(lambda: fill(give))
    pl.when(pl.program_id(0) == 1)(lambda: fill(own))


def wide_grad(at, lefts, rights):
    half = pl.BlockSpec((TOK, D // 2), lambda i, k, at: (0, lax.rem(i + 1 + at[1], 2)))
    column = lambda width: pl.BlockSpec((TOK, width), lambda i, k, at: (0, lax.rem(k + at[0], 4)))
    widths = [right.shape[1] // 4 for right in rights]
    total = sum(widths)
    return pl.pallas_call(
        functools.partial(wide_grad_body, len(lefts)),
        out_shape=[jax.ShapeDtypeStruct((4, D // 2, total), BF)] * 2,
        grid_spec=pltpu.PrefetchScalarGridSpec(
            num_scalar_prefetch=1,
            grid=(2, 4),
            in_specs=[half for _ in lefts] + [column(width) for width in widths],
            out_specs=[
                pl.BlockSpec((1, D // 2, total), lambda i, k, at: (k * i, 0, 0)),
                pl.BlockSpec((1, D // 2, total), lambda i, k, at: (k * (1 - i) + 3 * i, 0, 0)),
            ],
        ),
        compiler_params=pltpu.CompilerParams(vmem_limit_bytes=40 * MIB),
        cost_estimate=pl.CostEstimate(
            flops=8 * TOK * D * total, bytes_accessed=8 * D * total, transcendentals=0
        ),
        name="wide_grad",
    )(at, *lefts, *rights)


def spread_matrices():
    row = jnp.arange(384, dtype=jnp.int32)[:, None]
    column = jnp.arange(768, dtype=jnp.int32)[None, :]
    place = (column // 24) * 12 + column % 12
    late = (column % 24) // 12
    return jnp.stack([((row == place) & (late == h)).astype(BF) for h in range(2)])


def owner_grad_body(at, left, right, spread, own, give):
    width = right.shape[1] // 2
    rows = left[...]
    both = jnp.concatenate([dot(rows, spread[h], NN).astype(BF) for h in range(2)], axis=0)
    sides = jnp.concatenate([right[:, :width], right[:, width:]], axis=0)
    total = dot(both, sides, TN).astype(BF).reshape(32, 24, width)

    def fill(ref):
        ref[...] = total

    pl.when(pl.program_id(0) == 0)(lambda: fill(give))
    pl.when(pl.program_id(0) == 1)(lambda: fill(own))


def owner_grad(at, left, right, spread):
    width = right.shape[1] // 2
    return pl.pallas_call(
        owner_grad_body,
        out_shape=[jax.ShapeDtypeStruct((64, 24, width), BF)] * 2,
        grid_spec=pltpu.PrefetchScalarGridSpec(
            num_scalar_prefetch=1,
            grid=(2, 2),
            in_specs=[
                pl.BlockSpec((TOK, 384), lambda i, s, at: (0, lax.rem(i + 1 + at[1], 2) * 2 + s)),
                pl.BlockSpec((TOK, 2 * width), lambda i, s, at: (0, 0)),
                pl.BlockSpec((2, 384, 768), lambda i, s, at: (0, 0, 0)),
            ],
            out_specs=[
                pl.BlockSpec((32, 24, width), lambda i, s, at: (s * i, 0, 0)),
                pl.BlockSpec((32, 24, width), lambda i, s, at: (s * (1 - i) + i, 0, 0)),
            ],
        ),
        compiler_params=pltpu.CompilerParams(vmem_limit_bytes=40 * MIB),
        cost_estimate=pl.CostEstimate(
            flops=4 * TOK * D * 2 * width, bytes_accessed=4 * D * width, transcendentals=0
        ),
        name="owner_grad",
    )(at, left, right, spread)


beta_first = 0.9
beta_second = 0.95
adam_epsilon = 1e-08
gain_rate = 3.0
matrix_decay = 0.1
rope_base = 10000.0
ALL = ("dp", "context", "experts")
OWNERS = ("dp", "experts")
LINE = ("context", "experts")
Y_GROUPS = [[0, 1, 2, 3], [4, 5, 6, 7]]


def send_z(value, hop):
    pairs = [(z * 2 + h, ((z + hop) % 4) * 2 + h) for z in range(4) for h in range(2)]
    return lax.ppermute(value, "context", pairs)


def swap_xh(value):
    pairs = [(z * 2 + h, z * 2 + 1 - h) for z in range(4) for h in range(2)]
    return lax.ppermute(value, "context", pairs)


def send_y(value, hop):
    pairs = [(l * 4 + y, l * 4 + (y + hop) % 4) for l in range(2) for y in range(4)]
    return lax.ppermute(value, "experts", pairs)


def swap_xl(value):
    pairs = [(l * 4 + y, (1 - l) * 4 + y) for l in range(2) for y in range(4)]
    return lax.ppermute(value, "experts", pairs)


def swap_core(value):
    return lax.ppermute(value, "dp", [(0, 1), (1, 0)])


def place():
    context = lax.axis_index("context")
    experts = lax.axis_index("experts")
    return dict(d=lax.axis_index("dp"), z=context // 2, xh=context % 2, xl=experts // 4, y=experts % 4)


def ordered(flag, own, other):
    return jnp.where(flag == 0, jnp.stack([own, other]), jnp.stack([other, own]))


def keep_and_give(pair, flag):
    return (
        lax.dynamic_index_in_dim(pair, flag, 0, False),
        lax.dynamic_index_in_dim(pair, 1 - flag, 0, False),
    )


def rope_tables(positions):
    frequency = rope_base ** (jnp.arange(HD // 2, dtype=F32) * (-2.0 / HD))
    angles = positions.astype(F32)[:, None] * frequency[None, :]
    cosine, sine = jnp.cos(angles), jnp.sin(angles)
    return jnp.concatenate([cosine, cosine], axis=1), jnp.concatenate([-sine, sine], axis=1)


def adam_update(weight, first_moment, second_moment, gradient, step_rate, decay_term):
    first_new = beta_first * first_moment + (1.0 - beta_first) * gradient
    second_new = beta_second * second_moment + (1.0 - beta_second) * gradient * gradient
    first_hat = first_new / (1.0 - beta_first**STEP)
    second_hat = second_new / (1.0 - beta_second**STEP)
    weight_new = weight - step_rate * (
        first_hat / (jnp.sqrt(second_hat) + adam_epsilon) + decay_term * weight
    )
    return (weight_new, first_new, second_new)


def routing(ids, gates):
    flat = ids.reshape(-1)
    one_hot = (flat[:, None] == jnp.arange(EXPERTS, dtype=jnp.int32)).astype(jnp.int32)
    earlier = jnp.cumsum(one_hot, axis=0) - one_hot
    rank = jnp.sum(earlier * one_hot, axis=-1)
    owner = (flat % 2) * (EXPERTS // 2) + flat // 2
    slots = (owner * CAP + rank).reshape(ids.shape)
    hit = slots[:, :, None] == jnp.arange(ROWS, dtype=jnp.int32)
    pick = jnp.any(hit, axis=1).astype(BF)
    weight = jnp.sum(jnp.where(hit, gates[:, :, None], 0.0), axis=1)
    slot_gate = jnp.sum(weight, axis=0)[:, None]
    weight_high, weight_low = split(weight)
    return pick, pick.T, weight_high, weight_low, slot_gate


def exchange(rows):
    return lax.all_to_all(
        rows.reshape(EXPERTS, CAP, D), OWNERS, split_axis=0, concat_axis=0, tiled=True
    ).reshape(ROWS, D)


def gather_keys(rows):
    pair = ordered(place()["xh"], rows, swap_xh(rows))
    return [pair] + [send_z(pair, k) for k in (1, 2, 3)]


def return_keys(grads):
    total = grads[0].astype(F32)
    for k in (1, 2, 3):
        total = total + send_z(grads[k], -k).astype(F32)
    own, other = keep_and_give(total, place()["xh"])
    return own + swap_xh(other.astype(BF)).astype(F32)


def column_blocks(qkv_weight, out_weight):
    return jnp.concatenate(
        [
            qkv_weight.astype(BF).reshape(LAYERS, -1, 4, YQ),
            out_weight.astype(BF).transpose(0, 2, 1).reshape(LAYERS, -1, 4, YO),
        ],
        axis=-1,
    ).transpose(2, 0, 1, 3)


def core_pair(in_weight, down_weight):
    both = jnp.concatenate(
        [in_weight.astype(BF), down_weight.astype(BF).transpose(0, 2, 1)], axis=-1
    )
    own, give = keep_and_give(both, lax.axis_index("dp"))
    return own, swap_core(give)


def add_cores(grads):
    own, give = grads
    return (own.astype(F32) + swap_core(give).astype(F32)).astype(BF)


def wide_send(half):
    return [half[0]] + [send_y(half[k], k) for k in (1, 2, 3)]


def pack(rows, gains):
    high, low = split(gains)
    filled = jnp.zeros((rows.shape[0], 120), BF)
    return jnp.concatenate([rows.astype(BF), high, low, filled], axis=1)


def wide_sum(parts, gains=None):
    at = place()
    width = parts[0].shape[1]

    def packed(total):
        return pack(*total) if gains is not None else total[0].astype(BF)

    def unpacked(rows):
        rows = rows.astype(F32)
        if gains is None:
            return (rows,)
        return rows[:, :width], rows[:, width : width + 4] + rows[:, width + 4 : width + 8]

    def added(got):
        return tuple(sum(g[i] for g in got) for i in range(len(got[0])))

    total = (sum(part.astype(F32) for part in parts),) + (() if gains is None else (gains,))
    cut = packed(total).reshape(4, 192, -1)
    pieces = [lax.dynamic_index_in_dim(cut, (at["z"] + k) % 4, 0, False) for k in range(4)]
    total = added([unpacked(pieces[0])] + [unpacked(send_z(pieces[k], k)) for k in (1, 2, 3)])
    for flag, swap, rows in ((at["xh"], swap_xh, 96), (at["xl"], swap_xl, 48)):
        kept, other = keep_and_give(packed(total).reshape(2, rows, -1), flag)
        total = added([unpacked(kept), unpacked(swap(other))])
    cut = packed(total).reshape(4, 12, -1)
    pieces = [lax.dynamic_index_in_dim(cut, (at["y"] + k) % 4, 0, False) for k in range(4)]
    got = [unpacked(pieces[0])] + [unpacked(send_y(pieces[k], k)) for k in (1, 2, 3)]
    order = (at["y"] - jnp.arange(4, dtype=jnp.int32)) % 4
    last = jnp.take(jnp.stack([g[0] for g in got]), order, axis=0).transpose(1, 0, 2)
    return last if gains is None else (last, added(got)[1])


def owner_sum(parts):
    total = jnp.sum(parts.astype(F32), axis=0)
    return jnp.concatenate([total[:12], total[12:]], axis=1)


def scatter_experts(grads):
    pair = lax.psum_scatter(grads, "context", scatter_dimension=0)
    core = lax.axis_index("dp")
    own, give = keep_and_give(pair, core)
    return ordered(core, own, swap_core(give)).astype(F32)


def local(
    tokens,
    cotangent,
    expert_ids,
    gate_values,
    block_order,
    qkv_weight,
    qkv_first,
    qkv_second,
    out_weight,
    out_first,
    out_second,
    in_weight,
    in_first,
    in_second,
    down_weight,
    down_first,
    down_second,
    norm_gains,
    gain_first,
    gain_second,
):
    at = place()
    wide_at = jnp.stack([at["y"], at["d"]]).astype(jnp.int32)
    rows = lax.all_to_all(
        column_blocks(qkv_weight, out_weight),
        "experts",
        0,
        0,
        axis_index_groups=Y_GROUPS,
        tiled=True,
    )
    rows = rows.transpose(1, 0, 2, 3).reshape(LAYERS, 48, YQ + YO)
    projections = [
        lax.all_gather(rows[l], ALL, axis=0).reshape(32, 4, 1, 48, YQ + YO) for l in range(LAYERS)
    ]
    gain_rows = norm_gains.astype(BF).astype(F32).reshape(1, 1, 48)
    gains = lax.all_to_all(jnp.broadcast_to(gain_rows, (128, 1, 48)), ALL, 0, 0, tiled=True)
    gains = gains.reshape(128, 4, 12).transpose(1, 0, 2).reshape(4, 1, D)
    own, other = core_pair(in_weight[0], down_weight[0])
    column = [own] + [send_z(own, k) for k in (1, 2, 3)]
    beside = [swap_xh(part) for part in column]
    pair = ordered(at["xh"], other, swap_xh(other))
    pairs = [pair] + [send_z(pair, k) for k in (1, 2, 3)]
    later = ordered(at["d"], *core_pair(in_weight[1], down_weight[1]))
    gathered = lax.all_gather(later, "context", axis=0)
    turns = (at["z"] - jnp.arange(4, dtype=jnp.int32)) % 4
    both = jnp.arange(2, dtype=jnp.int32)
    chunk_places = jnp.concatenate(
        [
            at["d"] * 8 + turns * 2 + at["xh"],
            at["d"] * 8 + turns * 2 + 1 - at["xh"],
            ((1 - at["d"]) * 8 + turns[:, None] * 2 + both[None, :]).reshape(-1),
        ]
    ).astype(jnp.int32)
    gathered_places = (jnp.arange(8, dtype=jnp.int32)[:, None] + 8 * both[None, :]).reshape(-1)
    experts = [(column + beside + pairs, chunk_places), ([gathered], gathered_places)]

    order_row = block_order[0]
    offsets = jnp.arange(TOK, dtype=jnp.int32)
    places = jnp.arange(8, dtype=jnp.int32)
    source = (turns[:, None] * 2 + both[None, :]).reshape(-1)
    key_block = jnp.sum(jnp.where(source[:, None] == places, order_row, 0), axis=1)
    own_block = jnp.sum(jnp.where(places == lax.axis_index("context"), order_row, 0))
    query_pos = own_block * TOK + offsets
    key_pos = (key_block[:, None] * TOK + offsets[None, :]).reshape(-1, 1)
    cosine, sine = rope_tables(query_pos)
    query_pos = query_pos.reshape(1, -1)
    routes = [routing(expert_ids[l, 0], gate_values[l, 0]) for l in range(LAYERS)]
    spread = spread_matrices()
    cotangent_rows = (dot(routes[-1][1], cotangent[0], NN) * routes[-1][4]).astype(BF)
    start, last_owner = lax.optimization_barrier((tokens[0], exchange(cotangent_rows)))
    saved = []
    base, came_back = start, ()
    for l in range(LAYERS):
        pick, pick_t, weight_high, weight_low, slot_gate = routes[l]
        attn_in, scale_one, qkv, *rest = project(
            0, base, gains[2 * l], cosine, sine, projections[l], came_back
        )
        if l:
            base = rest[0]
        kv = gather_keys(qkv[:, QW:])
        mixed, level = attend(qkv, kv, key_pos, query_pos)
        middle, scale_two, sent = branch(
            0, base, mixed, gains[2 * l + 1], pick_t, projections[l]
        )
        received = exchange(sent)
        returned, hidden, act, slope = ffn(received, *experts[l])
        if l == 0:
            came_back = (exchange(returned), weight_high, weight_low)
        saved.append(
            (base, attn_in, scale_one, qkv, kv, mixed, level, middle, scale_two, received, hidden, act, slope)
        )
        base = middle
    d_out = cotangent[0]
    expert_sums = [None] * LAYERS
    gain_grads = [None] * (2 * LAYERS)
    for l in reversed(range(LAYERS)):
        (base, attn_in, scale_one, qkv, kv, mixed, level, middle, scale_two, received, hidden, act, slope) = (
            saved[l]
        )
        if l == LAYERS - 1:
            owner = last_owner
        else:
            owner, wide_half = lax.optimization_barrier((exchange(sent), wide_half))
            wide_parts = wide_send(wide_half)
        d_rows, d_both = ffn_back(owner, act, slope, *experts[l])
        came_grad, expert_grad = lax.optimization_barrier(
            (exchange(d_rows), ffn_grad(received, d_both, owner, hidden))
        )
        if l == LAYERS - 1:
            returned, came_grad = lax.optimization_barrier((returned, came_grad))
            returned = exchange(returned)
        else:
            expert_grad, expert_sums[l + 1] = lax.optimization_barrier(
                (expert_grad, expert_sums[l + 1])
            )
        expert_sums[l] = scatter_experts(expert_grad)
        d_base, d_branch, d_mixed, gain_grads[2 * l + 1] = branch_back(
            0,
            came_grad, routes[l][0], middle, scale_two, gains[2 * l + 1], d_out, projections[l]
        )
        if l == 0:
            out_half = add_cores(owner_grad(wide_at, d_branch, mixed, spread))
            out_parts = lax.all_to_all(out_half, LINE, 0, 0, tiled=True)
        d_queries, d_pairs = attend_back(qkv, kv, key_pos, query_pos, level, d_mixed)
        d_key_value = return_keys(d_pairs.reshape(4, 2, TOK, 2 * KW))
        if l == LAYERS - 1:
            d_key_value, returned = lax.optimization_barrier((d_key_value, returned))
            result = middle + dot(routes[l][2], returned, NN) + dot(routes[l][3], returned, NN)
        else:
            d_key_value, wide_parts[1], wide_parts[3] = lax.optimization_barrier(
                (d_key_value, wide_parts[1], wide_parts[3])
            )
        extra = (routes[l - 1][1], routes[l - 1][4]) if l else ()
        back = project_back(
            0,
            d_queries,
            d_key_value,
            cosine,
            sine,
            base,
            scale_one,
            gains[2 * l],
            d_base,
            projections[l],
            extra,
        )
        d_out, d_projected, gain_grads[2 * l] = back[:3]
        if l:
            sent = back[3]
            wide_half = add_cores(wide_grad(wide_at, [attn_in, d_branch], [d_projected, mixed]))
        else:
            qkv_half = add_cores(owner_grad(wide_at, attn_in, d_projected, spread))
            gain_rows = jnp.concatenate(gain_grads, axis=0).T.reshape(2, D // 2, 4)
            own, give = keep_and_give(gain_rows, at["d"])
            qkv_half, out_parts, wide_parts = lax.optimization_barrier(
                (qkv_half, out_parts, wide_parts)
            )
            qkv_parts = lax.all_to_all(qkv_half, LINE, 0, 0, tiled=True)
            wide_rows, gain_sum = wide_sum(wide_parts, own + swap_core(give))
    gain_sum = gain_sum.T.reshape(2, 2, 12)
    qkv_sum = jnp.stack([owner_sum(qkv_parts), wide_rows[:, :, :YQ].reshape(12, QKV)], axis=1)
    out_sum = jnp.stack([owner_sum(out_parts), wide_rows[:, :, YQ:].reshape(12, QW)], axis=1)
    in_sum = jnp.stack([s[:, :, : 2 * FF] for s in expert_sums])
    down_sum = jnp.stack([s[:, :, 2 * FF :] for s in expert_sums]).transpose(0, 1, 3, 2)
    wide_rate = 5.0 * D ** (-0.5)
    out_rate = 5.0 * (HQ * HD / 16.0) ** (-0.5)
    down_rate = 5.0 * (FF / 4.0) ** (-0.5)
    qkv_state = [v.transpose(1, 0, 2) for v in (qkv_weight, qkv_first, qkv_second)]
    out_state = [v.transpose(2, 0, 1) for v in (out_weight, out_first, out_second)]
    qkv_update = adam_update(*qkv_state, qkv_sum, wide_rate, matrix_decay)
    out_update = adam_update(*out_state, out_sum, out_rate, matrix_decay)
    updates = (
        tuple(v.transpose(1, 0, 2) for v in qkv_update)
        + tuple(v.transpose(1, 2, 0) for v in out_update)
        + adam_update(in_weight, in_first, in_second, in_sum, wide_rate, matrix_decay)
        + adam_update(down_weight, down_first, down_second, down_sum, down_rate, matrix_decay)
        + adam_update(norm_gains, gain_first, gain_second, gain_sum, gain_rate, 0.0)
    )
    return (result.astype(BF)[None], d_out[None]) + updates


def solution(mesh):
    rows = P(("dp", "experts"), "context", None)
    routes = P(None, ("dp", "experts"), "context", None)
    qkv = P(None, ALL, None)
    out = P(None, None, ALL)
    wide = P(None, "experts", ("dp", "context"), None)
    down = P(None, "experts", None, ("dp", "context"))
    states = (qkv,) * 3 + (out,) * 3 + (wide,) * 3 + (down,) * 3 + (out,) * 3
    return jax.shard_map(
        local,
        mesh=mesh,
        in_specs=(rows, rows, routes, routes, P(("dp", "experts"), None)) + states,
        out_specs=(rows, rows) + states,
        check_vma=False,
    )
```

```python
import functools
import itertools
import jax
import jax.numpy as jnp
from jax import lax
from jax.experimental import pallas as pl
from jax.experimental.pallas import tpu as pltpu
from jax.sharding import PartitionSpec as P

D = 1536
HQ = 12
HK = 2
HD = 128
FF = 768
TOP = 4
LAYERS = 2
STEP = 5
EXPERTS = 16
CAP = 40
ROWS = EXPERTS * CAP
QKV = (HQ + 2 * HK) * HD
QW = HQ * HD
KW = HK * HD
YQ = QKV // 4
YO = QW // 4
TOK = 128
KEYS = 1024
GROUP = HQ // HK
GT = GROUP * TOK
score_scale = HD ** (-0.5)
norm_epsilon = 1e-06
BF = jnp.bfloat16
F32 = jnp.float32
MIB = 1 << 20


def dot(a, b, contract):
    return lax.dot_general(a, b, (contract, ((), ())), preferred_element_type=F32)


NN = ((1,), (0,))
NT = ((1,), (1,))
TN = ((0,), (0,))


def split(value):
    high = value.astype(BF)
    return high, (value - high.astype(F32)).astype(BF)


def whole():
    return pl.BlockSpec(memory_space=pltpu.VMEM)


def scalars():
    return pl.BlockSpec(memory_space=pltpu.SMEM)


def anywhere():
    return pl.BlockSpec(memory_space=pltpu.HBM)


def call(body, outs, ins, specs, scratch, flops, moved, name, mib=40, out_specs=None, grid=None):
    return pl.pallas_call(
        body,
        out_shape=[jax.ShapeDtypeStruct(s, t) for s, t in outs],
        in_specs=specs,
        out_specs=out_specs or [whole() for _ in outs],
        scratch_shapes=scratch,
        grid=grid or (),
        compiler_params=pltpu.CompilerParams(vmem_limit_bytes=mib * MIB),
        cost_estimate=pl.CostEstimate(flops=int(flops), bytes_accessed=int(moved), transcendentals=0),
        name=name,
    )(*ins)


def turn(head, cosine, sine):
    return head * cosine + pltpu.roll(head, HD // 2, 1) * sine


def rope_heads(part, y, cosine, sine):
    heads = []
    for i in range(4):
        head = part[:, i * HD : (i + 1) * HD]
        heads.append(head if y == 3 and i >= 2 else turn(head, cosine, sine))
    return jnp.concatenate(heads, axis=1)


def load_parts(layer, w_ref, buf, sem, column, width):
    copies = [
        pltpu.make_async_copy(w_ref.at[:, y, layer, :, pl.ds(column, width)], buf.at[y], sem.at[y])
        for y in range(4)
    ]
    for copy in copies:
        copy.start()
    return copies


def with_parts(ins, weights, width):
    specs = [whole() for _ in ins] + [pl.BlockSpec(memory_space=pltpu.HBM)]
    scratch = [pltpu.VMEM((4, 32, 48, width), BF), pltpu.SemaphoreType.DMA((4,))]
    return list(ins) + [weights], specs, scratch


def cut(refs, count):
    return refs[:count], refs[count], refs[count + 1 : -2], refs[-2], refs[-1]


def project_body(layer, count, *refs):
    lead, w, outs, buf, sem = cut(refs, count)
    copies = load_parts(layer, w, buf, sem, 0, YQ)
    base, gain, cosine, sine = lead[:4]
    h = base[...].astype(F32)
    if count > 4:
        came, high, low = lead[4:]
        rows = came[...]
        h = h + (dot(high[...], rows, NN) + dot(low[...], rows, NN))
        outs[3][...] = h
    attn_in, scale, out = outs[:3]
    factor = lax.rsqrt(jnp.mean(h * h, axis=1, keepdims=True) + norm_epsilon)
    scale[...] = factor
    fed = (h * factor * gain[...]).astype(BF)
    attn_in[...] = fed
    for y in range(4):
        copies[y].wait()
        part = dot(fed, buf[y].reshape(D, -1), NN)
        out[:, y * YQ : (y + 1) * YQ] = rope_heads(part, y, cosine[...], sine[...]).astype(BF)


def project(layer, base, gain, cosine, sine, weights, extra=()):
    lead = [base, gain, cosine, sine, *extra]
    ins, specs, scratch = with_parts(lead, weights, YQ)
    outs = [((TOK, D), BF), ((TOK, 1), F32), ((TOK, QKV), BF)]
    if extra:
        outs = outs + [((TOK, D), F32)]
    return call(
        functools.partial(project_body, layer, len(lead)),
        outs,
        ins,
        specs,
        scratch,
        2 * TOK * D * QKV,
        2 * D * QKV + 8 * TOK * D,
        "project",
    )


def keep_keys(kv_refs, buf):
    for k, ref in enumerate(kv_refs):
        for h in range(2):
            buf[(2 * k + h) * TOK : (2 * k + h + 1) * TOK, :] = ref[h]


def stack_heads(ref, j):
    return jnp.concatenate(
        [ref[:, (j * GROUP + i) * HD : (j * GROUP + i + 1) * HD] for i in range(GROUP)], axis=0
    )


def unstack(total):
    return jnp.concatenate(
        [total[:, i * TOK : (i + 1) * TOK].T for i in range(GROUP)], axis=1
    )


def attend_body(qkv, kv0, kv1, kv2, kv3, key_pos, query_pos, mixed, norm, buf, keep):
    keep_keys((kv0, kv1, kv2, kv3), buf)
    places = jnp.concatenate([query_pos[...]] * GROUP, axis=1)
    for j in range(HK):
        queries = stack_heads(qkv, j)

        def score(b, top):
            at = pl.ds(pl.multiple_of(b * TOK, TOK), TOK)
            keys = buf[at, j * HD : (j + 1) * HD]
            values = dot(keys, queries, NT) * score_scale
            values = jnp.where(key_pos[at, :] <= places, values, -1e30)
            keep[at, :] = values
            return jnp.maximum(top, jnp.max(values, axis=0, keepdims=True))

        top = lax.fori_loop(0, KEYS // TOK, score, jnp.full((1, GT), -1e30, F32))

        def mix(b, carry):
            total, share = carry
            at = pl.ds(pl.multiple_of(b * TOK, TOK), TOK)
            e = jnp.exp(keep[at, :] - top)
            values = buf[at, KW + j * HD : KW + (j + 1) * HD]
            share = share + jnp.sum(e, axis=0, keepdims=True)
            return total + dot(values, e.astype(BF), TN), share

        total, share = lax.fori_loop(
            0, KEYS // TOK, mix, (jnp.zeros((HD, GT), F32), jnp.zeros((1, GT), F32))
        )
        norm[j : j + 1, :] = top + jnp.log(share)
        mixed[:, j * GT : (j + 1) * GT] = unstack(total / share).astype(BF)


def attend(qkv, kv, key_pos, query_pos):
    ins = [qkv, *kv, key_pos, query_pos]
    return call(
        attend_body,
        [((TOK, QW), BF), ((HK, GT), F32)],
        ins,
        [whole() for _ in ins],
        [pltpu.VMEM((KEYS, 2 * KW), BF), pltpu.VMEM((KEYS, GT), F32)],
        4 * TOK * KEYS * QW,
        2 * KEYS * 2 * KW,
        "attend",
    )


def attend_back_body(
    qkv, kv0, kv1, kv2, kv3, key_pos, query_pos, norm, d_mixed, d_queries, d_pairs, buf, kept, given
):
    keep_keys((kv0, kv1, kv2, kv3), buf)
    places = jnp.concatenate([query_pos[...]] * GROUP, axis=1)
    for j in range(HK):
        queries = stack_heads(qkv, j)
        upstream = stack_heads(d_mixed, j)
        level = norm[j : j + 1, :]

        def probs(b, delta):
            at = pl.ds(pl.multiple_of(b * TOK, TOK), TOK)
            keys = buf[at, j * HD : (j + 1) * HD]
            values = buf[at, KW + j * HD : KW + (j + 1) * HD]
            scores = dot(keys, queries, NT) * score_scale
            p = jnp.where(key_pos[at, :] <= places, jnp.exp(scores - level), 0.0)
            dp = dot(values, upstream, NT)
            kept[at, :] = p
            given[at, :] = dp
            d_pairs[at, KW + j * HD : KW + (j + 1) * HD] = dot(p.astype(BF), upstream, NN).astype(BF)
            return delta + jnp.sum(p * dp, axis=0, keepdims=True)

        delta = lax.fori_loop(0, KEYS // TOK, probs, jnp.zeros((1, GT), F32))

        def back(b, total):
            at = pl.ds(pl.multiple_of(b * TOK, TOK), TOK)
            keys = buf[at, j * HD : (j + 1) * HD]
            ds = (kept[at, :] * (given[at, :] - delta)).astype(BF)
            d_pairs[at, j * HD : (j + 1) * HD] = (dot(ds, queries, NN) * score_scale).astype(BF)
            return total + dot(keys, ds, TN)

        total = lax.fori_loop(0, KEYS // TOK, back, jnp.zeros((HD, GT), F32))
        d_queries[:, j * GT : (j + 1) * GT] = unstack(total * score_scale)


def attend_back(qkv, kv, key_pos, query_pos, norm, d_mixed):
    ins = [qkv, *kv, key_pos, query_pos, norm, d_mixed]
    return call(
        attend_back_body,
        [((TOK, QW), F32), ((KEYS, 2 * KW), BF)],
        ins,
        [whole() for _ in ins],
        [pltpu.VMEM((KEYS, 2 * KW), BF), pltpu.VMEM((KEYS, GT), F32), pltpu.VMEM((KEYS, GT), F32)],
        10 * TOK * KEYS * QW,
        4 * KEYS * 2 * KW,
        "attend_back",
    )


def branch_body(layer, *refs):
    (base, mixed, gain, pick), w, (hidden, scale, sent), buf, sem = cut(refs, 4)
    copies = load_parts(layer, w, buf, sem, YQ, YO)
    total = base[...].astype(F32)
    for y in range(4):
        copies[y].wait()
        total = total + dot(mixed[:, y * YO : (y + 1) * YO], buf[y].reshape(D, -1), NT)
    hidden[...] = total
    factor = lax.rsqrt(jnp.mean(total * total, axis=1, keepdims=True) + norm_epsilon)
    scale[...] = factor
    fed = (total * factor * gain[...]).astype(BF)
    sent[...] = dot(pick[...], fed, NN).astype(BF)


def branch(layer, base, mixed, gain, pick, weights):
    ins, specs, scratch = with_parts([base, mixed, gain, pick], weights, YO)
    return call(
        functools.partial(branch_body, layer),
        [((TOK, D), F32), ((TOK, 1), F32), ((ROWS, D), BF)],
        ins,
        specs,
        scratch,
        2 * TOK * D * QW + 2 * TOK * D * ROWS,
        2 * D * QW + 2 * ROWS * D,
        "branch",
    )


BLOCK = 320


def load_expert(w_refs, places, buf, sem):
    copies = []
    for ref in w_refs:
        lead = ref.shape[:-2]
        for at in itertools.product(*[range(n) for n in lead]):
            row = pl.multiple_of(places[len(copies)] * 96, 96)
            copies.append(
                pltpu.make_async_copy(
                    ref.at[at] if at else ref, buf.at[pl.ds(row, 96), :], sem.at[len(copies)]
                )
            )
    for copy in copies:
        copy.start()
    for copy in copies:
        copy.wait()


def gelu_parts(x):
    cdf = 0.5 * (1.0 + lax.erf(x * (0.5**0.5)))
    density = jnp.exp(-0.5 * x * x) * 0.3989422804014327
    return x * cdf, cdf + x * density


def ffn_body(n, places, received, *refs):
    w_refs, (returned, hidden, act, slope, buf, sem) = refs[:n], refs[n:]

    @pl.when(pl.program_id(0) == 0)
    def _():
        load_expert(w_refs, places, buf, sem)

    both = dot(received[...], buf[:, : 2 * FF], NN)
    up = both[:, FF:]
    gelu, gelu_slope = gelu_parts(both[:, :FF])
    low = (gelu * up).astype(BF)
    hidden[...] = low
    act[...] = gelu
    slope[...] = gelu_slope * up
    returned[...] = dot(low, buf[:, 2 * FF :], NT).astype(BF)


def row_block(width):
    return pl.BlockSpec((BLOCK, width), lambda i: (i, 0))


def ffn(received, w_list, places):
    return call(
        functools.partial(ffn_body, len(w_list)),
        [((ROWS, D), BF), ((ROWS, FF), BF), ((ROWS, FF), F32), ((ROWS, FF), F32)],
        [places, received, *w_list],
        [scalars(), row_block(D)] + [anywhere() for _ in w_list],
        [pltpu.VMEM((D, 3 * FF), BF), pltpu.SemaphoreType.DMA((16,))],
        2 * ROWS * D * 3 * FF,
        2 * D * 3 * FF + 16 * ROWS * FF,
        "ffn",
        out_specs=[row_block(D), row_block(FF), row_block(FF), row_block(FF)],
        grid=(ROWS // BLOCK,),
    )


def ffn_back_body(n, places, owner, act, slope, *refs):
    w_refs, (d_rows, d_both, buf, sem) = refs[:n], refs[n:]

    @pl.when(pl.program_id(0) == 0)
    def _():
        load_expert(w_refs, places, buf, sem)

    d_hidden = dot(owner[...], buf[:, 2 * FF :], NN)
    both = jnp.concatenate([d_hidden * slope[...], d_hidden * act[...]], axis=1).astype(BF)
    d_both[...] = both
    d_rows[...] = dot(both, buf[:, : 2 * FF], NT).astype(BF)


def ffn_back(owner, act, slope, w_list, places):
    return call(
        functools.partial(ffn_back_body, len(w_list)),
        [((ROWS, D), BF), ((ROWS, 2 * FF), BF)],
        [places, owner, act, slope, *w_list],
        [scalars(), row_block(D), row_block(FF), row_block(FF)] + [anywhere() for _ in w_list],
        [pltpu.VMEM((D, 3 * FF), BF), pltpu.SemaphoreType.DMA((16,))],
        2 * ROWS * D * 3 * FF,
        2 * D * 3 * FF + 16 * ROWS * FF,
        "ffn_back",
        out_specs=[row_block(D), row_block(2 * FF)],
        grid=(ROWS // BLOCK,),
    )


def ffn_grad_body(received, d_both, owner, hidden, out):
    out[:, 0, :, : 2 * FF] = dot(received[...], d_both[...], TN).astype(BF).reshape(8, 96, 2 * FF)
    out[:, 0, :, 2 * FF :] = dot(owner[...], hidden[...], TN).astype(BF).reshape(8, 96, FF)


def ffn_grad(received, d_both, owner, hidden):
    half = pl.BlockSpec((ROWS, D // 2), lambda i: (0, i))
    fixed = lambda width: pl.BlockSpec((ROWS, width), lambda i: (0, 0))
    return call(
        ffn_grad_body,
        [((8, 2, 96, 3 * FF), BF)],
        [received, d_both, owner, hidden],
        [half, fixed(2 * FF), half, fixed(FF)],
        [],
        2 * ROWS * D * 3 * FF,
        2 * D * 3 * FF + 8 * ROWS * D,
        "ffn_grad",
        out_specs=[pl.BlockSpec((8, 1, 96, 3 * FF), lambda i: (0, i, 0, 0))],
        grid=(2,),
    )[0]


def norm_back(upstream, rows, factor, gain):
    normed = rows * factor
    scaled = upstream * gain
    return (
        factor * (scaled - normed * jnp.mean(scaled * normed, axis=1, keepdims=True)),
        jnp.sum(upstream * normed, axis=0, keepdims=True),
    )


def branch_back_body(layer, *refs):
    lead, w, outs, buf, sem = cut(refs, 6)
    source, pick_t, base, scale, gain, d_out = lead
    d_base, low, d_mixed, d_gain = outs
    copies = load_parts(layer, w, buf, sem, YQ, YO)
    d_fed = dot(pick_t[...], source[...], NN)
    term, d_gain[...] = norm_back(d_fed, base[...], scale[...], gain[...])
    total = d_out[...].astype(F32) + term
    d_base[...] = total
    rounded = total.astype(BF)
    low[...] = rounded
    for y in range(4):
        copies[y].wait()
        d_mixed[:, y * YO : (y + 1) * YO] = dot(rounded, buf[y].reshape(D, -1), NN).astype(BF)


def branch_back(layer, source, pick_t, base, scale, gain, d_out, weights):
    ins, specs, scratch = with_parts([source, pick_t, base, scale, gain, d_out], weights, YO)
    return call(
        functools.partial(branch_back_body, layer),
        [((TOK, D), F32), ((TOK, D), BF), ((TOK, QW), BF), ((1, D), F32)],
        ins,
        specs,
        scratch,
        2 * TOK * D * QW + 2 * TOK * D * ROWS,
        2 * D * QW + 2 * ROWS * D,
        "branch_back",
    )


def project_back_body(layer, count, *refs):
    lead, w, outs, buf, sem = cut(refs, count)
    dq, dkv, cosine, sine, base, scale, gain, d_out = lead[:8]
    d_base, d_proj, d_gain = outs[:3]
    copies = load_parts(layer, w, buf, sem, 0, YQ)
    total = jnp.zeros((TOK, D), F32)
    for y in range(4):
        part = dq[:, y * YQ : (y + 1) * YQ] if y < 3 else dkv[...]
        rounded = rope_heads(part, y, cosine[...], -sine[...]).astype(BF)
        d_proj[:, y * YQ : (y + 1) * YQ] = rounded
        copies[y].wait()
        total = total + dot(rounded, buf[y].reshape(D, -1), NT)
    term, d_gain[...] = norm_back(total, base[...].astype(F32), scale[...], gain[...])
    d_hidden = d_out[...] + term
    d_base[...] = d_hidden
    if count > 8:
        pick, gate = lead[8:]
        high, low = split(d_hidden)
        rows = dot(pick[...], high, NN) + dot(pick[...], low, NN)
        outs[3][...] = (rows * gate[...]).astype(BF)


def project_back(layer, dq, dkv, cosine, sine, base, scale, gain, d_out, weights, extra=()):
    lead = [dq, dkv, cosine, sine, base, scale, gain, d_out, *extra]
    ins, specs, scratch = with_parts(lead, weights, YQ)
    outs = [((TOK, D), F32), ((TOK, QKV), BF), ((1, D), F32)]
    if extra:
        outs = outs + [((ROWS, D), BF)]
    return call(
        functools.partial(project_back_body, layer, len(lead)),
        outs,
        ins,
        specs,
        scratch,
        2 * TOK * D * QKV,
        2 * D * QKV + 8 * TOK * D,
        "project_back",
    )


def wide_grad_body(count, at, *refs):
    own, give = refs[-2:]

    def fill(ref):
        column = 0
        for left, right in zip(refs[:count], refs[count : 2 * count]):
            width = right.shape[1]
            ref[0, :, column : column + width] = dot(left[...], right[...], TN).astype(BF)
            column += width

    pl.when(pl.program_id(0) == 0)(lambda: fill(give))
    pl.when(pl.program_id(0) == 1)(lambda: fill(own))


def wide_grad(at, lefts, rights):
    half = pl.BlockSpec((TOK, D // 2), lambda i, k, at: (0, lax.rem(i + 1 + at[1], 2)))
    column = lambda width: pl.BlockSpec((TOK, width), lambda i, k, at: (0, lax.rem(k + at[0], 4)))
    widths = [right.shape[1] // 4 for right in rights]
    total = sum(widths)
    return pl.pallas_call(
        functools.partial(wide_grad_body, len(lefts)),
        out_shape=[jax.ShapeDtypeStruct((4, D // 2, total), BF)] * 2,
        grid_spec=pltpu.PrefetchScalarGridSpec(
            num_scalar_prefetch=1,
            grid=(2, 4),
            in_specs=[half for _ in lefts] + [column(width) for width in widths],
            out_specs=[
                pl.BlockSpec((1, D // 2, total), lambda i, k, at: (k * i, 0, 0)),
                pl.BlockSpec((1, D // 2, total), lambda i, k, at: (k * (1 - i) + 3 * i, 0, 0)),
            ],
        ),
        compiler_params=pltpu.CompilerParams(vmem_limit_bytes=40 * MIB),
        cost_estimate=pl.CostEstimate(
            flops=8 * TOK * D * total, bytes_accessed=8 * D * total, transcendentals=0
        ),
        name="wide_grad",
    )(at, *lefts, *rights)


def spread_matrices():
    row = jnp.arange(384, dtype=jnp.int32)[:, None]
    column = jnp.arange(768, dtype=jnp.int32)[None, :]
    place = (column // 24) * 12 + column % 12
    late = (column % 24) // 12
    return jnp.stack([((row == place) & (late == h)).astype(BF) for h in range(2)])


def owner_grad_body(at, left, right, spread, own, give):
    width = right.shape[1] // 2
    rows = left[...]
    both = jnp.concatenate([dot(rows, spread[h], NN).astype(BF) for h in range(2)], axis=0)
    sides = jnp.concatenate([right[:, :width], right[:, width:]], axis=0)
    total = dot(both, sides, TN).astype(BF).reshape(32, 24, width)

    def fill(ref):
        ref[...] = total

    pl.when(pl.program_id(0) == 0)(lambda: fill(give))
    pl.when(pl.program_id(0) == 1)(lambda: fill(own))


def owner_grad(at, left, right, spread):
    width = right.shape[1] // 2
    return pl.pallas_call(
        owner_grad_body,
        out_shape=[jax.ShapeDtypeStruct((64, 24, width), BF)] * 2,
        grid_spec=pltpu.PrefetchScalarGridSpec(
            num_scalar_prefetch=1,
            grid=(2, 2),
            in_specs=[
                pl.BlockSpec((TOK, 384), lambda i, s, at: (0, lax.rem(i + 1 + at[1], 2) * 2 + s)),
                pl.BlockSpec((TOK, 2 * width), lambda i, s, at: (0, 0)),
                pl.BlockSpec((2, 384, 768), lambda i, s, at: (0, 0, 0)),
            ],
            out_specs=[
                pl.BlockSpec((32, 24, width), lambda i, s, at: (s * i, 0, 0)),
                pl.BlockSpec((32, 24, width), lambda i, s, at: (s * (1 - i) + i, 0, 0)),
            ],
        ),
        compiler_params=pltpu.CompilerParams(vmem_limit_bytes=40 * MIB),
        cost_estimate=pl.CostEstimate(
            flops=4 * TOK * D * 2 * width, bytes_accessed=4 * D * width, transcendentals=0
        ),
        name="owner_grad",
    )(at, left, right, spread)


beta_first = 0.9
beta_second = 0.95
adam_epsilon = 1e-08
gain_rate = 3.0
matrix_decay = 0.1
rope_base = 10000.0
ALL = ("dp", "context", "experts")
OWNERS = ("dp", "experts")
LINE = ("context", "experts")
Y_GROUPS = [[0, 1, 2, 3], [4, 5, 6, 7]]


def send_z(value, hop):
    pairs = [(z * 2 + h, ((z + hop) % 4) * 2 + h) for z in range(4) for h in range(2)]
    return lax.ppermute(value, "context", pairs)


def swap_xh(value):
    pairs = [(z * 2 + h, z * 2 + 1 - h) for z in range(4) for h in range(2)]
    return lax.ppermute(value, "context", pairs)


def send_y(value, hop):
    pairs = [(l * 4 + y, l * 4 + (y + hop) % 4) for l in range(2) for y in range(4)]
    return lax.ppermute(value, "experts", pairs)


def swap_xl(value):
    pairs = [(l * 4 + y, (1 - l) * 4 + y) for l in range(2) for y in range(4)]
    return lax.ppermute(value, "experts", pairs)


def swap_core(value):
    return lax.ppermute(value, "dp", [(0, 1), (1, 0)])


def place():
    context = lax.axis_index("context")
    experts = lax.axis_index("experts")
    return dict(d=lax.axis_index("dp"), z=context // 2, xh=context % 2, xl=experts // 4, y=experts % 4)


def ordered(flag, own, other):
    return jnp.where(flag == 0, jnp.stack([own, other]), jnp.stack([other, own]))


def keep_and_give(pair, flag):
    return (
        lax.dynamic_index_in_dim(pair, flag, 0, False),
        lax.dynamic_index_in_dim(pair, 1 - flag, 0, False),
    )


def rope_tables(positions):
    frequency = rope_base ** (jnp.arange(HD // 2, dtype=F32) * (-2.0 / HD))
    angles = positions.astype(F32)[:, None] * frequency[None, :]
    cosine, sine = jnp.cos(angles), jnp.sin(angles)
    return jnp.concatenate([cosine, cosine], axis=1), jnp.concatenate([-sine, sine], axis=1)


def adam_update(weight, first_moment, second_moment, gradient, step_rate, decay_term):
    first_new = beta_first * first_moment + (1.0 - beta_first) * gradient
    second_new = beta_second * second_moment + (1.0 - beta_second) * gradient * gradient
    first_hat = first_new / (1.0 - beta_first**STEP)
    second_hat = second_new / (1.0 - beta_second**STEP)
    weight_new = weight - step_rate * (
        first_hat / (jnp.sqrt(second_hat) + adam_epsilon) + decay_term * weight
    )
    return (weight_new, first_new, second_new)


def routing(ids, gates):
    flat = ids.reshape(-1)
    one_hot = (flat[:, None] == jnp.arange(EXPERTS, dtype=jnp.int32)).astype(jnp.int32)
    earlier = jnp.cumsum(one_hot, axis=0) - one_hot
    rank = jnp.sum(earlier * one_hot, axis=-1)
    owner = (flat % 2) * (EXPERTS // 2) + flat // 2
    slots = (owner * CAP + rank).reshape(ids.shape)
    hit = slots[:, :, None] == jnp.arange(ROWS, dtype=jnp.int32)
    pick = jnp.any(hit, axis=1).astype(BF)
    weight = jnp.sum(jnp.where(hit, gates[:, :, None], 0.0), axis=1)
    slot_gate = jnp.sum(weight, axis=0)[:, None]
    weight_high, weight_low = split(weight)
    return pick, pick.T, weight_high, weight_low, slot_gate


def exchange(rows):
    return lax.all_to_all(
        rows.reshape(EXPERTS, CAP, D), OWNERS, split_axis=0, concat_axis=0, tiled=True
    ).reshape(ROWS, D)


def gather_keys(rows):
    pair = ordered(place()["xh"], rows, swap_xh(rows))
    return [pair] + [send_z(pair, k) for k in (1, 2, 3)]


def return_keys(grads):
    total = grads[0].astype(F32)
    for k in (1, 2, 3):
        total = total + send_z(grads[k], -k).astype(F32)
    own, other = keep_and_give(total, place()["xh"])
    return own + swap_xh(other.astype(BF)).astype(F32)


def column_blocks(qkv_weight, out_weight):
    return jnp.concatenate(
        [
            qkv_weight.astype(BF).reshape(LAYERS, -1, 4, YQ),
            out_weight.astype(BF).transpose(0, 2, 1).reshape(LAYERS, -1, 4, YO),
        ],
        axis=-1,
    ).transpose(2, 0, 1, 3)


def core_pair(in_weight, down_weight):
    both = jnp.concatenate(
        [in_weight.astype(BF), down_weight.astype(BF).transpose(0, 2, 1)], axis=-1
    )
    own, give = keep_and_give(both, lax.axis_index("dp"))
    return own, swap_core(give)


def add_cores(grads):
    own, give = grads
    return (own.astype(F32) + swap_core(give).astype(F32)).astype(BF)


def wide_send(half):
    return [half[0]] + [send_y(half[k], k) for k in (1, 2, 3)]


def pack(rows, gains):
    high, low = split(gains)
    filled = jnp.zeros((rows.shape[0], 120), BF)
    return jnp.concatenate([rows.astype(BF), high, low, filled], axis=1)


def wide_sum(parts, gains=None):
    at = place()
    width = parts[0].shape[1]

    def packed(total):
        return pack(*total) if gains is not None else total[0].astype(BF)

    def unpacked(rows):
        rows = rows.astype(F32)
        if gains is None:
            return (rows,)
        return rows[:, :width], rows[:, width : width + 4] + rows[:, width + 4 : width + 8]

    def added(got):
        return tuple(sum(g[i] for g in got) for i in range(len(got[0])))

    total = (sum(part.astype(F32) for part in parts),) + (() if gains is None else (gains,))
    cut = packed(total).reshape(4, 192, -1)
    pieces = [lax.dynamic_index_in_dim(cut, (at["z"] + k) % 4, 0, False) for k in range(4)]
    total = added([unpacked(pieces[0])] + [unpacked(send_z(pieces[k], k)) for k in (1, 2, 3)])
    for flag, swap, rows in ((at["xh"], swap_xh, 96), (at["xl"], swap_xl, 48)):
        kept, other = keep_and_give(packed(total).reshape(2, rows, -1), flag)
        total = added([unpacked(kept), unpacked(swap(other))])
    cut = packed(total).reshape(4, 12, -1)
    pieces = [lax.dynamic_index_in_dim(cut, (at["y"] + k) % 4, 0, False) for k in range(4)]
    got = [unpacked(pieces[0])] + [unpacked(send_y(pieces[k], k)) for k in (1, 2, 3)]
    order = (at["y"] - jnp.arange(4, dtype=jnp.int32)) % 4
    last = jnp.take(jnp.stack([g[0] for g in got]), order, axis=0).transpose(1, 0, 2)
    return last if gains is None else (last, added(got)[1])


def owner_sum(parts):
    total = jnp.sum(parts.astype(F32), axis=0)
    return jnp.concatenate([total[:12], total[12:]], axis=1)


def scatter_experts(grads):
    pair = lax.psum_scatter(grads, "context", scatter_dimension=0)
    core = lax.axis_index("dp")
    own, give = keep_and_give(pair, core)
    return ordered(core, own, swap_core(give)).astype(F32)


def local(
    tokens,
    cotangent,
    expert_ids,
    gate_values,
    block_order,
    qkv_weight,
    qkv_first,
    qkv_second,
    out_weight,
    out_first,
    out_second,
    in_weight,
    in_first,
    in_second,
    down_weight,
    down_first,
    down_second,
    norm_gains,
    gain_first,
    gain_second,
):
    at = place()
    wide_at = jnp.stack([at["y"], at["d"]]).astype(jnp.int32)
    rows = lax.all_to_all(
        column_blocks(qkv_weight, out_weight),
        "experts",
        0,
        0,
        axis_index_groups=Y_GROUPS,
        tiled=True,
    )
    rows = rows.transpose(1, 0, 2, 3).reshape(LAYERS, 48, YQ + YO)
    projections = [
        lax.all_gather(rows[l], ALL, axis=0).reshape(32, 4, 1, 48, YQ + YO) for l in range(LAYERS)
    ]
    gain_rows = norm_gains.astype(BF).astype(F32).reshape(1, 1, 48)
    gains = lax.all_to_all(jnp.broadcast_to(gain_rows, (128, 1, 48)), ALL, 0, 0, tiled=True)
    gains = gains.reshape(128, 4, 12).transpose(1, 0, 2).reshape(4, 1, D)
    own, other = core_pair(in_weight[0], down_weight[0])
    column = [own] + [send_z(own, k) for k in (1, 2, 3)]
    beside = [swap_xh(part) for part in column]
    pair = ordered(at["xh"], other, swap_xh(other))
    pairs = [pair] + [send_z(pair, k) for k in (1, 2, 3)]
    later = ordered(at["d"], *core_pair(in_weight[1], down_weight[1]))
    gathered = lax.all_gather(later, "context", axis=0)
    turns = (at["z"] - jnp.arange(4, dtype=jnp.int32)) % 4
    both = jnp.arange(2, dtype=jnp.int32)
    chunk_places = jnp.concatenate(
        [
            at["d"] * 8 + turns * 2 + at["xh"],
            at["d"] * 8 + turns * 2 + 1 - at["xh"],
            ((1 - at["d"]) * 8 + turns[:, None] * 2 + both[None, :]).reshape(-1),
        ]
    ).astype(jnp.int32)
    gathered_places = (jnp.arange(8, dtype=jnp.int32)[:, None] + 8 * both[None, :]).reshape(-1)
    experts = [(column + beside + pairs, chunk_places), ([gathered], gathered_places)]

    order_row = block_order[0]
    offsets = jnp.arange(TOK, dtype=jnp.int32)
    places = jnp.arange(8, dtype=jnp.int32)
    source = (turns[:, None] * 2 + both[None, :]).reshape(-1)
    key_block = jnp.sum(jnp.where(source[:, None] == places, order_row, 0), axis=1)
    own_block = jnp.sum(jnp.where(places == lax.axis_index("context"), order_row, 0))
    query_pos = own_block * TOK + offsets
    key_pos = (key_block[:, None] * TOK + offsets[None, :]).reshape(-1, 1)
    cosine, sine = rope_tables(query_pos)
    query_pos = query_pos.reshape(1, -1)
    routes = [routing(expert_ids[l, 0], gate_values[l, 0]) for l in range(LAYERS)]
    spread = spread_matrices()
    cotangent_rows = (dot(routes[-1][1], cotangent[0], NN) * routes[-1][4]).astype(BF)
    start, last_owner = lax.optimization_barrier((tokens[0], exchange(cotangent_rows)))
    saved = []
    base, came_back = start, ()
    for l in range(LAYERS):
        pick, pick_t, weight_high, weight_low, slot_gate = routes[l]
        attn_in, scale_one, qkv, *rest = project(
            0, base, gains[2 * l], cosine, sine, projections[l], came_back
        )
        if l:
            base = rest[0]
        kv = gather_keys(qkv[:, QW:])
        mixed, level = attend(qkv, kv, key_pos, query_pos)
        middle, scale_two, sent = branch(
            0, base, mixed, gains[2 * l + 1], pick_t, projections[l]
        )
        received = exchange(sent)
        returned, hidden, act, slope = ffn(received, *experts[l])
        if l == 0:
            came_back = (exchange(returned), weight_high, weight_low)
        saved.append(
            (base, attn_in, scale_one, qkv, kv, mixed, level, middle, scale_two, received, hidden, act, slope)
        )
        base = middle
    d_out = cotangent[0]
    expert_sums = [None] * LAYERS
    gain_grads = [None] * (2 * LAYERS)
    for l in reversed(range(LAYERS)):
        (base, attn_in, scale_one, qkv, kv, mixed, level, middle, scale_two, received, hidden, act, slope) = (
            saved[l]
        )
        if l == LAYERS - 1:
            owner = last_owner
        else:
            owner, wide_half = lax.optimization_barrier((exchange(sent), wide_half))
            wide_parts = wide_send(wide_half)
        d_rows, d_both = ffn_back(owner, act, slope, *experts[l])
        came_grad, expert_grad = lax.optimization_barrier(
            (exchange(d_rows), ffn_grad(received, d_both, owner, hidden))
        )
        if l == LAYERS - 1:
            returned, came_grad = lax.optimization_barrier((returned, came_grad))
            returned = exchange(returned)
        else:
            expert_grad, expert_sums[l + 1] = lax.optimization_barrier(
                (expert_grad, expert_sums[l + 1])
            )
        expert_sums[l] = scatter_experts(expert_grad)
        d_base, d_branch, d_mixed, gain_grads[2 * l + 1] = branch_back(
            0,
            came_grad, routes[l][0], middle, scale_two, gains[2 * l + 1], d_out, projections[l]
        )
        if l == 0:
            out_half = add_cores(owner_grad(wide_at, d_branch, mixed, spread))
            out_parts = lax.all_to_all(out_half, LINE, 0, 0, tiled=True)
        d_queries, d_pairs = attend_back(qkv, kv, key_pos, query_pos, level, d_mixed)
        d_key_value = return_keys(d_pairs.reshape(4, 2, TOK, 2 * KW))
        if l == LAYERS - 1:
            d_key_value, returned = lax.optimization_barrier((d_key_value, returned))
            result = middle + dot(routes[l][2], returned, NN) + dot(routes[l][3], returned, NN)
        else:
            d_key_value, wide_parts = lax.optimization_barrier((d_key_value, wide_parts))
        extra = (routes[l - 1][1], routes[l - 1][4]) if l else ()
        back = project_back(
            0,
            d_queries,
            d_key_value,
            cosine,
            sine,
            base,
            scale_one,
            gains[2 * l],
            d_base,
            projections[l],
            extra,
        )
        d_out, d_projected, gain_grads[2 * l] = back[:3]
        if l:
            sent = back[3]
            wide_half = add_cores(wide_grad(wide_at, [attn_in, d_branch], [d_projected, mixed]))
        else:
            qkv_half = add_cores(owner_grad(wide_at, attn_in, d_projected, spread))
            gain_rows = jnp.concatenate(gain_grads, axis=0).T.reshape(2, D // 2, 4)
            own, give = keep_and_give(gain_rows, at["d"])
            qkv_half, out_parts = lax.optimization_barrier((qkv_half, out_parts))
            qkv_parts = lax.all_to_all(qkv_half, LINE, 0, 0, tiled=True)
            wide_rows, gain_sum = wide_sum(wide_parts, own + swap_core(give))
    gain_sum = gain_sum.T.reshape(2, 2, 12)
    qkv_sum = jnp.stack([owner_sum(qkv_parts), wide_rows[:, :, :YQ].reshape(12, QKV)], axis=1)
    out_sum = jnp.stack([owner_sum(out_parts), wide_rows[:, :, YQ:].reshape(12, QW)], axis=1)
    in_sum = jnp.stack([s[:, :, : 2 * FF] for s in expert_sums])
    down_sum = jnp.stack([s[:, :, 2 * FF :] for s in expert_sums]).transpose(0, 1, 3, 2)
    wide_rate = 5.0 * D ** (-0.5)
    out_rate = 5.0 * (HQ * HD / 16.0) ** (-0.5)
    down_rate = 5.0 * (FF / 4.0) ** (-0.5)
    qkv_state = [v.transpose(1, 0, 2) for v in (qkv_weight, qkv_first, qkv_second)]
    out_state = [v.transpose(2, 0, 1) for v in (out_weight, out_first, out_second)]
    qkv_update = adam_update(*qkv_state, qkv_sum, wide_rate, matrix_decay)
    out_update = adam_update(*out_state, out_sum, out_rate, matrix_decay)
    updates = (
        tuple(v.transpose(1, 0, 2) for v in qkv_update)
        + tuple(v.transpose(1, 2, 0) for v in out_update)
        + adam_update(in_weight, in_first, in_second, in_sum, wide_rate, matrix_decay)
        + adam_update(down_weight, down_first, down_second, down_sum, down_rate, matrix_decay)
        + adam_update(norm_gains, gain_first, gain_second, gain_sum, gain_rate, 0.0)
    )
    return (result.astype(BF)[None], d_out[None]) + updates


def solution(mesh):
    rows = P(("dp", "experts"), "context", None)
    routes = P(None, ("dp", "experts"), "context", None)
    qkv = P(None, ALL, None)
    out = P(None, None, ALL)
    wide = P(None, "experts", ("dp", "context"), None)
    down = P(None, "experts", None, ("dp", "context"))
    states = (qkv,) * 3 + (out,) * 3 + (wide,) * 3 + (down,) * 3 + (out,) * 3
    return jax.shard_map(
        local,
        mesh=mesh,
        in_specs=(rows, rows, routes, routes, P(("dp", "experts"), None)) + states,
        out_specs=(rows, rows) + states,
        check_vma=False,
    )
```
